32 devices in a mesh: roll: 16 (over z, y, core), rep: 2 (over x).
Axes of the slice: x: 2, y: 2, z: 4, core: 2. Of those that a mesh axis runs over, the one named last changes fastest.
Arguments:
- rollout: bfloat16 [65536, 256], P(('roll', 'rep')), may hold values from -7.8 to 7.8
- demo: bfloat16 [32768, 256], P('roll'), may hold values from -6 to 6
- projection: bfloat16 [256, 256], replicated, may hold values from -0.375 to 0.375
- location: int32 [256], replicated, may hold values from 0 to 255, as said below
- pair_block: int32 [512, 8], P(('roll', 'rep')), may hold values from 0 to 255, as said below
- pair_count: int32 [512], P(('roll', 'rep')), may hold values from 1 to 8, as said below
Outputs:
- reward: float32 [65536], P(('roll', 'rep'))
- rollout_potential: float32 [65536], P(('roll', 'rep'))
- demo_potential: float32 [32768], P('roll')
The draws below stay inside these ranges and needn't reach their ends.
Inputs may be any that keep to these rules, and one draw needn't show every extreme that they name: location is a permutation; demonstration block d is stored block location[d], held by roll index location[d] // 16. `pair_block`: among the slots in use of the 16 rollout blocks of one device, at most 8 name blocks stored on any one roll index, and some device reaches 8. `pair_count`: on one roll index every rollout block uses all 8 slots.
All inputs are finite; a program needn't handle non-finite values.
Results may differ from the reference program's by a relative error of at most 0.0024.
Values may be sent and summed in bfloat16 or wider, within the bound.
A program may use at most 128 MiB of HBM per device.

```python
import jax
import jax.numpy as jnp
from jax import lax

E = 256
BLK = 128
PAIRS = 8
ITERS = 2
RBD = 16
DBD = 16
NRB = 512
NDB = 256
ROLL_FRAMES = 65536
DEMO_FRAMES = 32768
N_ROLL = 16
N_REP = 2


def demo_places(key):
    return jax.random.permutation(jax.random.fold_in(key, 7), NDB).astype(jnp.int32)


def draw_rollout(key, part):
    noise = jnp.clip(jax.random.normal(jax.random.fold_in(key, 31), (ROLL_FRAMES, E), jnp.float32), -6.0, 6.0)
    devices = NRB // RBD
    rank_keys = jax.random.split(jax.random.fold_in(key, 37), devices)
    ranks = jax.vmap(lambda subkey: jax.random.permutation(subkey, RBD))(rank_keys).astype(jnp.float32)
    offsets = jax.random.uniform(jax.random.fold_in(key, 41), (devices, RBD), jnp.float32)
    signs = jnp.where(jax.random.bernoulli(jax.random.fold_in(key, 43), 0.5, (devices, RBD)), 1.0, -1.0)
    levels = 1.8 * (ranks + offsets) / RBD * signs
    shift = jnp.repeat(levels.reshape(NRB), BLK, total_repeat_length=ROLL_FRAMES)
    return (noise + shift[:, None]).astype(jnp.bfloat16)


def draw_location(key, part):
    return demo_places(key)


def draw_pair_block(key, part):
    places = demo_places(key)
    inverse = jnp.zeros((NDB,), jnp.int32).at[places].set(jnp.arange(NDB, dtype=jnp.int32))
    devices = NRB // RBD
    slot_count = RBD * PAIRS
    owner_keys = jax.random.split(jax.random.fold_in(key, 13), devices)
    owners = jax.vmap(lambda subkey: jax.random.permutation(subkey, N_ROLL).astype(jnp.int32))(owner_keys)
    slot_owner = jnp.arange(slot_count, dtype=jnp.int32) % N_ROLL
    owner_roll = owners[:, slot_owner]
    local_block = jax.random.randint(jax.random.fold_in(key, 17), (devices, slot_count), 0, DBD).astype(jnp.int32)
    chosen = inverse[owner_roll * DBD + local_block]
    return chosen.reshape(NRB, PAIRS).astype(jnp.int32)


def draw_pair_count(key, part):
    counts = jax.random.randint(jax.random.fold_in(key, 23), (NRB,), 1, PAIRS + 1).astype(jnp.int32)
    chosen_roll = jax.random.randint(jax.random.fold_in(key, 29), (), 0, N_ROLL).astype(jnp.int32)
    roll_of = jnp.arange(NRB, dtype=jnp.int32) // (RBD * N_REP)
    return jnp.where(roll_of == chosen_roll, PAIRS, counts).astype(jnp.int32)


def steps_of(own_key, dims, shards, smallest, top_value):
    gain = 1.0
    for position, shards_of in shards:
        steps = jax.random.uniform(jax.random.fold_in(jax.random.fold_in(own_key, 6), position), (shards_of,), jnp.float32, smallest / len(shards), top_value / len(shards))
        gain = gain * jnp.repeat(jnp.exp(steps), dims[position] // shards_of).reshape((-1,) + (1,) * (len(dims) - 1 - position))
    return gain


def bell_draw(stream_key, extent, scale, bound, shards=(), held_as=jnp.bfloat16):
    values = scale * jax.random.normal(stream_key, extent, jnp.float32)
    if shards:
        values = values * steps_of(stream_key, extent, shards, -0.22, 0.18)
    return jnp.clip(values, -bound, bound).astype(held_as)


def setup_inputs(seed: int = 0) -> dict:
    streams_of = jax.random.split(jax.random.key(seed), 7)
    return {
        "rollout": draw_rollout(jax.random.fold_in(streams_of[6], 71), 0),
        "demo": bell_draw(streams_of[1], (DEMO_FRAMES, E), 1.0, 6.0, ((0, 16),)),
        "projection": bell_draw(streams_of[2], (E, E), E ** -0.5, 0.375),
        "location": draw_location(jax.random.fold_in(streams_of[6], 71), 0),
        "pair_block": draw_pair_block(jax.random.fold_in(streams_of[6], 71), 0),
        "pair_count": draw_pair_count(jax.random.fold_in(streams_of[6], 71), 0),
    }


EPSILON = 0.02
UNMATCHED = 2.0
SLACK = -100.0
NEGLIGIBLE = -1.0e30


def reference(rollout, demo, projection, location, pair_block, pair_count):
    roll_count = pair_block.shape[0]
    pair_slots = pair_block.shape[1]
    demo_count = location.shape[0]
    block_len = rollout.shape[0] // roll_count
    features = projection.shape[1]
    roll_codes = jnp.dot(rollout, projection, preferred_element_type=jnp.float32).astype(jnp.bfloat16)
    demo_codes = jnp.dot(demo, projection, preferred_element_type=jnp.float32).astype(jnp.bfloat16)
    roll_tiles = roll_codes.reshape(roll_count, block_len, features)
    demo_tiles = demo_codes.reshape(demo_count, block_len, features)
    stored = location[pair_block].astype(jnp.int32)
    active = jnp.arange(pair_slots, dtype=jnp.int32)[None, :] < pair_count[:, None]
    group_size = RBD
    groups = roll_count // group_size
    group_ids = jnp.arange(groups, dtype=jnp.int32)

    def costs_of(group_index):
        start = (group_index * group_size).astype(jnp.int32)
        rows_x = lax.dynamic_slice_in_dim(roll_tiles, start, group_size, 0).astype(jnp.float32)
        targets = lax.dynamic_slice_in_dim(stored, start, group_size, 0)
        rows_y = demo_tiles[targets].astype(jnp.float32)
        crossed = jnp.einsum("gie,gpje->gpij", rows_x, rows_y)
        norm_x = jnp.sum(rows_x * rows_x, axis=2)
        norm_y = jnp.sum(rows_y * rows_y, axis=3)
        return (norm_x[:, None, :, None] + norm_y[:, :, None, :] - 2.0 * crossed) / features

    def column_pass(roll_pot):
        def per_group(group_index):
            costs = costs_of(group_index)
            start = (group_index * group_size).astype(jnp.int32)
            pots = lax.dynamic_slice_in_dim(roll_pot, start, group_size, 0)
            scores = (pots[:, None, :, None] - costs) / EPSILON
            largest = jnp.max(scores, axis=2)
            return largest + jnp.log(jnp.sum(jnp.exp(scores - largest[:, :, None, :]), axis=2))

        partials = lax.map(per_group, group_ids).reshape(roll_count * pair_slots, block_len)
        segment_ids = jnp.where(active, stored, demo_count).reshape(-1).astype(jnp.int32)
        largest = jax.ops.segment_max(partials, segment_ids, num_segments=demo_count + 1)[:demo_count]
        highest = jnp.maximum(largest, SLACK)
        padded = jnp.concatenate([highest, jnp.zeros((1, block_len), highest.dtype)], axis=0)
        summed = jax.ops.segment_sum(jnp.exp(partials - padded[segment_ids]), segment_ids, num_segments=demo_count + 1)[:demo_count]
        log_total = highest + jnp.log(summed + jnp.exp(SLACK - highest))
        return -EPSILON * log_total

    def row_pass(demo_pot):
        def per_group(group_index):
            costs = costs_of(group_index)
            start = (group_index * group_size).astype(jnp.int32)
            targets = lax.dynamic_slice_in_dim(stored, start, group_size, 0)
            in_use = lax.dynamic_slice_in_dim(active, start, group_size, 0)
            pots = demo_pot[targets]
            scores = (pots[:, :, None, :] - costs) / EPSILON
            scores = jnp.where(in_use[:, :, None, None], scores, NEGLIGIBLE)
            largest = jnp.maximum(jnp.max(scores, axis=(1, 3)), SLACK)
            summed = jnp.sum(jnp.exp(scores - largest[:, None, :, None]), axis=(1, 3)) + jnp.exp(SLACK - largest)
            log_total = largest + jnp.log(summed)
            weights = jnp.exp(scores - log_total[:, None, :, None])
            reward = -(jnp.sum(weights * costs, axis=(1, 3)) + jnp.exp(SLACK - log_total) * UNMATCHED)
            return -EPSILON * log_total, reward

        potentials, rewards = lax.map(per_group, group_ids)
        return potentials.reshape(roll_count, block_len), rewards.reshape(roll_count, block_len)

    roll_pot = jnp.zeros((roll_count, block_len), jnp.float32)
    demo_pot = jnp.zeros((demo_count, block_len), jnp.float32)
    reward = jnp.zeros((roll_count, block_len), jnp.float32)
    for iteration in range(ITERS):
        demo_pot = column_pass(roll_pot)
        roll_pot, reward = row_pass(demo_pot)
    return reward.reshape(-1), roll_pot.reshape(-1), demo_pot.reshape(-1)
```

```python
import functools
import math

import jax
import jax.numpy as jnp
from jax import lax
from jax.experimental import pallas as pl
from jax.experimental.pallas import tpu as pltpu
from jax.sharding import PartitionSpec as P

EPSILON = 0.02
UNMATCHED = 2.0
SLACK = -100.0
LOG2E = math.log2(math.e)
SCALE = LOG2E / EPSILON
SHIFT = 50.0 * LOG2E
FLOOR = math.exp(SLACK + 50.0)
UNROLL = 4


def pass_kernel(kind, total_ref, home_ref, target_ref, u_ref, v_ref, unorm_ref, vnorm_ref, pot_ref, *rest):
    roll_blocks, blk = unorm_ref.shape
    feats = u_ref.shape[1]
    unit = SCALE / feats
    if kind == "column":
        out_ref, row_term, col_acc = rest
        col_acc[...] = jnp.zeros_like(col_acc)
    elif kind == "row":
        out_ref, row_term, col_term, acc = rest
        acc[...] = jnp.zeros_like(acc)
    else:
        out_ref, row_term, col_term, acc, wacc = rest
        acc[...] = jnp.zeros_like(acc)
        wacc[...] = jnp.zeros_like(wacc)

    def prepare(b, carry):
        line = unorm_ref[pl.ds(b, 1), :] * (-unit)
        if kind == "column":
            line = line + (pot_ref[pl.ds(b, 1), :] + SHIFT)
        row_term[pl.ds(b * blk, blk), :] = jnp.transpose(jnp.broadcast_to(line, (blk, blk)))
        return carry

    lax.fori_loop(0, roll_blocks, prepare, 0)
    if kind != "column":
        col_term[...] = pot_ref[...] + SHIFT

    total = total_ref[0]

    def step(k, carry):
        parts = []
        for p in range(UNROLL):
            at = k * UNROLL + p
            b = home_ref[at]
            t = target_ref[at]
            live = jnp.where(at < total, 0.0, -1e30)
            rows = pl.ds(pl.multiple_of(b * blk, blk), blk)
            crossed = lax.dot_general(
                u_ref[rows, :],
                v_ref[pl.ds(pl.multiple_of(t * blk, blk), blk), :],
                (((1,), (1,)), ((), ())),
                preferred_element_type=jnp.float32,
            )
            y = crossed * (2.0 * unit) + row_term[rows, :]
            line = vnorm_ref[pl.ds(t, 1), :] * (-unit)
            if kind == "column":
                e = jnp.exp2(y + (line + live))
                parts.append((t, jnp.sum(e.reshape(blk // 8, 8, blk), axis=0)))
            elif kind == "row":
                e = jnp.exp2(y + (line + (col_term[pl.ds(t, 1), :] + live)))
                parts.append((rows, e))
            else:
                y = y + line
                e = jnp.exp2(y + (col_term[pl.ds(t, 1), :] + live))
                parts.append((rows, e, e * y))
        for part in parts:
            if kind == "column":
                at8 = pl.ds(pl.multiple_of(part[0] * 8, 8), 8)
                col_acc[at8, :] = col_acc[at8, :] + part[1]
            else:
                acc[part[0], :] = acc[part[0], :] + part[1]
                if kind == "final":
                    wacc[part[0], :] = wacc[part[0], :] + part[2]
        return carry

    lax.fori_loop(0, (total + UNROLL - 1) // UNROLL, step, 0)

    if kind == "column":
        targets = out_ref.shape[0]
        out_ref[...] = jnp.sum(col_acc[...].reshape(targets, 8, blk), axis=1)
    else:

        def finish(b, carry):
            rows = pl.ds(pl.multiple_of(b * blk, blk), blk)
            out_ref[0, pl.ds(b, 1), :] = jnp.sum(jnp.transpose(acc[rows, :]), axis=0, keepdims=True)
            if kind == "final":
                out_ref[1, pl.ds(b, 1), :] = jnp.sum(
                    jnp.transpose(wacc[rows, :]), axis=0, keepdims=True
                ) * (-1.0 / SCALE)
            return carry

        lax.fori_loop(0, roll_blocks, finish, 0)


def run_pass(kind, lists, u, v, unorm, vnorm, pot):
    roll_blocks, blk = unorm.shape
    targets = vnorm.shape[0]
    smem = pl.BlockSpec(memory_space=pltpu.SMEM)
    vmem = pl.BlockSpec(memory_space=pltpu.VMEM)
    frames = pltpu.VMEM((roll_blocks * blk, blk), jnp.float32)
    if kind == "column":
        out = jax.ShapeDtypeStruct((targets, blk), jnp.float32)
        scratch = [frames, pltpu.VMEM((targets * 8, blk), jnp.float32)]
    else:
        out = jax.ShapeDtypeStruct((2 if kind == "final" else 1, roll_blocks, blk), jnp.float32)
        scratch = [frames, pltpu.VMEM((targets, blk), jnp.float32), frames]
        if kind == "final":
            scratch.append(frames)
    pairs = lists[1].shape[0] // 2
    return pl.pallas_call(
        functools.partial(pass_kernel, kind),
        out_shape=out,
        in_specs=[smem] * 3 + [vmem] * 5,
        out_specs=vmem,
        scratch_shapes=scratch,
        compiler_params=pltpu.CompilerParams(vmem_limit_bytes=56 * 1024 * 1024),
        cost_estimate=pl.CostEstimate(
            flops=2 * pairs * blk * blk * u.shape[1],
            bytes_accessed=2 * (u.size + v.size),
            transcendentals=pairs * blk * blk,
        ),
        name="pass_" + kind,
    )(*lists, u, v, unorm, vnorm, pot)


def listed(pair_block, pair_count, location, demo_count, share, part):
    roll_blocks, slots = pair_block.shape
    n = roll_blocks * slots
    names = jnp.arange(location.shape[0], dtype=jnp.int32)
    flat = pair_block.reshape(n)
    stored = jnp.sum(jnp.where(flat[:, None] == names[None, :], location[None, :], 0), axis=1)
    active = (jnp.arange(slots, dtype=jnp.int32)[None, :] < pair_count[:, None]).reshape(n)
    local = stored % demo_count
    mine = active & (local // share == part)
    target = (stored // demo_count) * share + local % share
    ids = jnp.arange(n, dtype=jnp.int32)
    rank = jnp.sum((mine[None, :] & (ids[None, :] < ids[:, None])).astype(jnp.int32), axis=1)
    place = jnp.where(mine, rank, -1)
    hit = place[None, :] == ids[:, None]
    home = jnp.sum(jnp.where(hit, (ids // slots)[None, :], 0), axis=1)
    target = jnp.sum(jnp.where(hit, target[None, :], 0), axis=1)
    total = jnp.sum(mine.astype(jnp.int32)).reshape(1)
    return total, jnp.pad(home, (0, UNROLL)), jnp.pad(target, (0, UNROLL))


def project(frames, projection):
    return jnp.dot(frames, projection, preferred_element_type=jnp.float32).astype(jnp.bfloat16)


def norms(codes, blk):
    wide = codes.astype(jnp.float32)
    return jnp.sum(wide * wide, axis=1).reshape(-1, blk)


def body(rollout, demo, projection, location, pair_block, pair_count):
    own_blocks = pair_block.shape[0]
    blk = rollout.shape[0] // own_blocks
    demo_count = demo.shape[0] // blk
    reps = lax.axis_size("rep")
    part = lax.axis_index("rep")
    share = demo_count // reps
    lists = listed(
        lax.all_gather(pair_block, "rep", tiled=True),
        lax.all_gather(pair_count, "rep", tiled=True),
        location,
        demo_count,
        share,
        part,
    )
    own_demo = lax.dynamic_slice_in_dim(demo, part * (share * blk), share * blk, 0)
    own_v = project(own_demo, projection)
    own_u = project(rollout, projection)
    v = lax.all_gather(own_v, "roll", tiled=True)
    vnorm = lax.all_gather(norms(own_v, blk), "roll", tiled=True)
    u = lax.all_gather(own_u, "rep", tiled=True)
    unorm = lax.all_gather(norms(own_u, blk), "rep", tiled=True)

    roll_pot = jnp.zeros_like(unorm)
    for iteration in range(2):
        sums = run_pass("column", lists, u, v, unorm, vnorm, roll_pot)
        demo_pot = SHIFT - jnp.log2(lax.psum(sums, "roll") + FLOOR)
        kind = "final" if iteration == 1 else "row"
        sums = run_pass(kind, lists, u, v, unorm, vnorm, demo_pot)
        sums = lax.psum(sums, "rep")
        heights = sums[0] + FLOOR
        roll_pot = SHIFT - jnp.log2(heights)
    reward = -(sums[1] + UNMATCHED * FLOOR) / heights
    mine = lax.axis_index("roll") * share
    own_pot = lax.all_gather(lax.dynamic_slice_in_dim(demo_pot, mine, share, 0), "rep", tiled=True)
    first = part * own_blocks
    return (
        lax.dynamic_slice_in_dim(reward, first, own_blocks, 0).reshape(-1),
        lax.dynamic_slice_in_dim(roll_pot, first, own_blocks, 0).reshape(-1) / SCALE,
        own_pot.reshape(-1) / SCALE,
    )


def solution(mesh):
    placed = (
        P(("roll", "rep"), None),
        P("roll", None),
        P(),
        P(),
        P(("roll", "rep"), None),
        P(("roll", "rep")),
    )
    return jax.shard_map(
        body,
        mesh=mesh,
        in_specs=placed,
        out_specs=(P(("roll", "rep")), P(("roll", "rep")), P("roll")),
        check_vma=False,
    )
```

```python
import functools
import math

import jax
import jax.numpy as jnp
from jax import lax
from jax.experimental import pallas as pl
from jax.experimental.pallas import tpu as pltpu
from jax.sharding import PartitionSpec as P

EPSILON = 0.02
UNMATCHED = 2.0
SLACK = -100.0
LOG2E = math.log2(math.e)
SCALE = LOG2E / EPSILON
SHIFT = 50.0 * LOG2E
FLOOR = math.exp(SLACK + 50.0)
UNROLL = 4
DIRECT = 16
MESH = pl.DeviceIdType.MESH


def pass_kernel(kind, total_ref, home_ref, target_ref, u_ref, v_ref, unorm_ref, vnorm_ref, pot_ref, *rest):
    roll_blocks, blk = unorm_ref.shape
    feats = u_ref.shape[1]
    unit = SCALE / feats
    if kind == "column":
        out_ref, row_term, col_acc = rest
        col_acc[...] = jnp.zeros_like(col_acc)
    elif kind == "row":
        out_ref, row_term, col_term, acc = rest
        acc[...] = jnp.zeros_like(acc)
    else:
        out_ref, row_term, col_term, acc, wacc = rest
        acc[...] = jnp.zeros_like(acc)
        wacc[...] = jnp.zeros_like(wacc)

    def prepare(b, carry):
        line = unorm_ref[pl.ds(b, 1), :] * (-unit)
        if kind == "column":
            line = line + (pot_ref[pl.ds(b, 1), :] + SHIFT)
        row_term[pl.ds(b * blk, blk), :] = jnp.transpose(jnp.broadcast_to(line, (blk, blk)))
        return carry

    lax.fori_loop(0, roll_blocks, prepare, 0)
    if kind != "column":
        col_term[...] = pot_ref[...] + SHIFT

    total = total_ref[0]

    def step(k, carry):
        parts = []
        for p in range(UNROLL):
            at = k * UNROLL + p
            b = home_ref[at]
            t = target_ref[at]
            live = jnp.where(at < total, 0.0, -1e30)
            rows = pl.ds(pl.multiple_of(b * blk, blk), blk)
            crossed = lax.dot_general(
                u_ref[rows, :],
                v_ref[pl.ds(pl.multiple_of(t * blk, blk), blk), :],
                (((1,), (1,)), ((), ())),
                preferred_element_type=jnp.float32,
            )
            y = crossed * (2.0 * unit) + row_term[rows, :]
            line = vnorm_ref[pl.ds(t, 1), :] * (-unit)
            if kind == "column":
                e = jnp.exp2(y + (line + live))
                parts.append((t, jnp.sum(e.reshape(blk // 8, 8, blk), axis=0)))
            elif kind == "row":
                e = jnp.exp2(y + (line + (col_term[pl.ds(t, 1), :] + live)))
                parts.append((rows, e))
            else:
                y = y + line
                e = jnp.exp2(y + (col_term[pl.ds(t, 1), :] + live))
                parts.append((rows, e, e * y))
        for part in parts:
            if kind == "column":
                at8 = pl.ds(pl.multiple_of(part[0] * 8, 8), 8)
                col_acc[at8, :] = col_acc[at8, :] + part[1]
            else:
                acc[part[0], :] = acc[part[0], :] + part[1]
                if kind == "final":
                    wacc[part[0], :] = wacc[part[0], :] + part[2]
        return carry

    lax.fori_loop(0, (total + UNROLL - 1) // UNROLL, step, 0)

    if kind == "column":
        targets = out_ref.shape[0]
        out_ref[...] = jnp.sum(col_acc[...].reshape(targets, 8, blk), axis=1)
    else:

        def finish(b, carry):
            rows = pl.ds(pl.multiple_of(b * blk, blk), blk)
            out_ref[0, pl.ds(b, 1), :] = jnp.sum(jnp.transpose(acc[rows, :]), axis=0, keepdims=True)
            if kind == "final":
                out_ref[1, pl.ds(b, 1), :] = jnp.sum(
                    jnp.transpose(wacc[rows, :]), axis=0, keepdims=True
                ) * (-1.0 / SCALE)
            return carry

        lax.fori_loop(0, roll_blocks, finish, 0)


def run_pass(kind, lists, u, v, unorm, vnorm, pot):
    roll_blocks, blk = unorm.shape
    targets = vnorm.shape[0]
    smem = pl.BlockSpec(memory_space=pltpu.SMEM)
    vmem = pl.BlockSpec(memory_space=pltpu.VMEM)
    frames = pltpu.VMEM((roll_blocks * blk, blk), jnp.float32)
    if kind == "column":
        out = jax.ShapeDtypeStruct((targets, blk), jnp.float32)
        scratch = [frames, pltpu.VMEM((targets * 8, blk), jnp.float32)]
    else:
        out = jax.ShapeDtypeStruct((2 if kind == "final" else 1, roll_blocks, blk), jnp.float32)
        scratch = [frames, pltpu.VMEM((targets, blk), jnp.float32), frames]
        if kind == "final":
            scratch.append(frames)
    pairs = lists[1].shape[0] // 2
    return pl.pallas_call(
        functools.partial(pass_kernel, kind),
        out_shape=out,
        in_specs=[smem] * 3 + [vmem] * 5,
        out_specs=vmem,
        scratch_shapes=scratch,
        compiler_params=pltpu.CompilerParams(vmem_limit_bytes=56 * 1024 * 1024),
        cost_estimate=pl.CostEstimate(
            flops=2 * pairs * blk * blk * u.shape[1],
            bytes_accessed=2 * (u.size + v.size),
            transcendentals=pairs * blk * blk,
        ),
        name="pass_" + kind,
    )(*lists, u, v, unorm, vnorm, pot)


def listed(pair_block, pair_count, location, demo_count, share, part):
    roll_blocks, slots = pair_block.shape
    n = roll_blocks * slots
    names = jnp.arange(location.shape[0], dtype=jnp.int32)
    flat = pair_block.reshape(n)
    stored = jnp.sum(jnp.where(flat[:, None] == names[None, :], location[None, :], 0), axis=1)
    active = (jnp.arange(slots, dtype=jnp.int32)[None, :] < pair_count[:, None]).reshape(n)
    local = stored % demo_count
    mine = active & (local // share == part)
    target = (stored // demo_count) * share + local % share
    ids = jnp.arange(n, dtype=jnp.int32)
    rank = jnp.sum((mine[None, :] & (ids[None, :] < ids[:, None])).astype(jnp.int32), axis=1)
    place = jnp.where(mine, rank, -1)
    hit = place[None, :] == ids[:, None]
    home = jnp.sum(jnp.where(hit, (ids // slots)[None, :], 0), axis=1)
    target = jnp.sum(jnp.where(hit, target[None, :], 0), axis=1)
    total = jnp.sum(mine.astype(jnp.int32)).reshape(1)
    return total, jnp.pad(home, (0, UNROLL)), jnp.pad(target, (0, UNROLL))


def project(frames, projection):
    return jnp.dot(frames, projection, preferred_element_type=jnp.float32).astype(jnp.bfloat16)


def norms(codes, blk):
    wide = codes.astype(jnp.float32)
    return jnp.sum(wide * wide, axis=1).reshape(-1, blk)


def greet(partners):
    barrier = pltpu.get_barrier_semaphore()
    for partner in partners:
        pl.semaphore_signal(barrier, inc=1, device_id=partner, device_id_type=MESH)
    pl.semaphore_wait(barrier, len(partners))


def others(axis, size):
    me = lax.axis_index(axis)
    return [{axis: lax.rem(me + d, size)} for d in range(1, size)]


def gather_kernel(n, reps, *refs):
    own_v, own_vnorm, own_u, own_unorm, own_pairs = refs[:5]
    v, vnorm, u, unorm, pairs = refs[5:10]
    ring_send, ring_recv, side_send, side_recv, norm_send, norm_recv, rep_send, rep_recv, home = refs[10:]
    me = lax.axis_index("roll")
    part = lax.axis_index("rep")
    chips = n // 2
    hops = chips // 2
    core = lax.rem(me, 2)
    chip = me // 2
    odd = lax.rem(chip, 2)
    place = (1 - odd) * (chip // 2) + odd * (chips - 1 - chip // 2)

    def at_place(p):
        p = lax.rem(p + 2 * chips, chips)
        high = p // hops
        return ((1 - high) * (2 * p) + high * (2 * (chips - 1 - p) + 1)) * 2 + core

    twin = {"roll": me + 1 - 2 * core}
    ways = ({"roll": at_place(place + 1)}, {"roll": at_place(place - 1)})
    rows = own_v.shape[0] // 2
    greet(others("roll", n) + others("rep", reps))

    waits = []
    arrivals = []

    def origin(way, s):
        return at_place(place - s) if way == 0 else at_place(place + s)

    def chunk(s, way, half):
        piece = pl.ds(half * rows, rows)
        if s == 0:
            return own_v.at[piece], v.at[me, piece]
        block = origin(way, s)
        return v.at[block, piece], v.at[block, piece]

    def send(s, way, half):
        source, target = chunk(s, way, half)
        copy = pltpu.make_async_remote_copy(
            src_ref=source, dst_ref=target,
            send_sem=ring_send.at[way, s, half], recv_sem=ring_recv.at[way, s, half],
            device_id=ways[way], device_id_type=MESH,
        )
        copy.start()
        return copy

    def cross(s, way, half):
        source, target = chunk(s, way, half)
        copy = pltpu.make_async_remote_copy(
            src_ref=source, dst_ref=target,
            send_sem=side_send.at[way, s, half], recv_sem=side_recv.at[way, s, half],
            device_id=twin, device_id_type=MESH,
        )
        copy.start()
        waits.append(copy)

    def travels(s, way, half):
        return s < hops - 1 or (s == hops - 1 and half == way)

    moving = {}
    for half in range(2):
        for way in range(2):
            if travels(0, way, half):
                moving[0, way, half] = send(0, way, half)
    for source, targets, axis, which, sends, recvs in (
        (own_pairs, pairs, "rep", 0, rep_send, rep_recv),
        (own_unorm, unorm, "rep", 1, rep_send, rep_recv),
        (own_u, u, "rep", 2, rep_send, rep_recv),
        (own_vnorm, vnorm, "roll", 0, norm_send, norm_recv),
    ):
        index = part if axis == "rep" else me
        for d, partner in enumerate(others(axis, reps if axis == "rep" else n)):
            copy = pltpu.make_async_remote_copy(
                src_ref=source, dst_ref=targets.at[index],
                send_sem=sends.at[which, d], recv_sem=recvs.at[which, d],
                device_id=partner, device_id_type=MESH,
            )
            copy.start()
            waits.append(copy)
    for half in range(2):
        cross(0, 0, half)
    stays = []
    for k, (source, target) in enumerate(
        ((own_v, v.at[me]), (own_vnorm, vnorm.at[me]), (own_u, u.at[part]), (own_unorm, unorm.at[part]), (own_pairs, pairs.at[part]))
    ):
        copy = pltpu.make_async_copy(source, target, home.at[k])
        copy.start()
        stays.append(copy)
    for s in range(1, hops + 1):
        for half in range(2):
            for way in range(2):
                if (s - 1, way, half) not in moving:
                    continue
                moving[s - 1, way, half].wait_recv()
                if travels(s, way, half):
                    moving[s, way, half] = send(s, way, half)
                cross(s, way, half)
    for copy in moving.values():
        copy.wait_send()
    for copy in stays:
        copy.wait()
    for copy in waits:
        copy.wait()


def gathered(n, reps, own_v, own_vnorm, own_u, own_unorm, own_pairs):
    hops = n // 4
    own = (own_v, own_vnorm, own_u, own_unorm, own_pairs)
    counts = (n, n, reps, reps, reps)
    anywhere = pl.BlockSpec(memory_space=pl.ANY)
    dma = pltpu.SemaphoreType.DMA
    return pl.pallas_call(
        functools.partial(gather_kernel, n, reps),
        out_shape=[jax.ShapeDtypeStruct((c,) + a.shape, a.dtype) for c, a in zip(counts, own)],
        in_specs=[anywhere] * 5,
        out_specs=[anywhere] * 5,
        scratch_shapes=[
            dma((2, hops, 2)), dma((2, hops, 2)),
            dma((2, hops + 1, 2)), dma((2, hops + 1, 2)),
            dma((1, n - 1)), dma((1, n - 1)),
            dma((3, reps - 1)), dma((3, reps - 1)),
            dma((5,)),
        ],
        compiler_params=pltpu.CompilerParams(collective_id=0, has_side_effects=True),
        name="gather_codes",
    )(*own)


def column_kernel(n, sums, out, landed, full, first_send, first_recv, second_send, second_recv):
    me = lax.axis_index("roll")
    partners = others("roll", n)
    greet(partners)
    copies = []
    for d, partner in enumerate(partners):
        copy = pltpu.make_async_remote_copy(
            src_ref=sums.at[partner["roll"]], dst_ref=landed.at[d],
            send_sem=first_send.at[d], recv_sem=first_recv.at[d],
            device_id=partner, device_id_type=MESH,
        )
        copy.start()
        copies.append(copy)
    total = sums[me]
    for d, copy in enumerate(copies):
        copy.wait_recv()
        total = total + landed[d]
    full[me] = SHIFT - jnp.log2(total + FLOOR)
    seconds = []
    for d, partner in enumerate(partners):
        copy = pltpu.make_async_remote_copy(
            src_ref=full.at[me], dst_ref=full.at[me],
            send_sem=second_send.at[d], recv_sem=second_recv.at[d],
            device_id=partner, device_id_type=MESH,
        )
        copy.start()
        seconds.append(copy)
    for copy in copies:
        copy.wait_send()
    for copy in seconds:
        copy.wait()
    out[...] = full[...]


def column_potentials(n, sums, call):
    if n > DIRECT:
        return SHIFT - jnp.log2(lax.psum(sums, "roll") + FLOOR)
    share, blk = sums.shape[0] // n, sums.shape[1]
    sums = sums.reshape(n, share, blk)
    dma = pltpu.SemaphoreType.DMA((n - 1,))
    vmem = pl.BlockSpec(memory_space=pltpu.VMEM)
    out = pl.pallas_call(
        functools.partial(column_kernel, n),
        out_shape=jax.ShapeDtypeStruct(sums.shape, sums.dtype),
        in_specs=[vmem],
        out_specs=vmem,
        scratch_shapes=[
            pltpu.VMEM((n - 1, share, blk), jnp.float32),
            pltpu.VMEM((n, share, blk), jnp.float32),
            dma, dma, dma, dma,
        ],
        compiler_params=pltpu.CompilerParams(collective_id=1 + call, has_side_effects=True),
        name="column_exchange_%d" % call,
    )(sums)
    return out.reshape(n * share, blk)


def row_kernel(reps, sums, out, landed, send_sem, recv_sem):
    partners = others("rep", reps)
    greet(partners)
    copies = []
    for d, partner in enumerate(partners):
        copy = pltpu.make_async_remote_copy(
            src_ref=sums, dst_ref=landed.at[d], send_sem=send_sem.at[d], recv_sem=recv_sem.at[d],
            device_id=partner, device_id_type=MESH,
        )
        copy.start()
        copies.append(copy)
    total = sums[...]
    for d, copy in enumerate(copies):
        copy.wait_recv()
        total = total + landed[d]
    out[...] = total
    for copy in copies:
        copy.wait_send()


def row_totals(reps, sums, call):
    dma = pltpu.SemaphoreType.DMA((reps - 1,))
    vmem = pl.BlockSpec(memory_space=pltpu.VMEM)
    return pl.pallas_call(
        functools.partial(row_kernel, reps),
        out_shape=jax.ShapeDtypeStruct(sums.shape, sums.dtype),
        in_specs=[vmem],
        out_specs=vmem,
        scratch_shapes=[pltpu.VMEM((reps - 1,) + sums.shape, jnp.float32), dma, dma],
        compiler_params=pltpu.CompilerParams(collective_id=3 + call, has_side_effects=True),
        name="row_exchange_%d" % call,
    )(sums)


def body(rollout, demo, projection, location, pair_block, pair_count):
    own_blocks, slots = pair_block.shape
    blk = rollout.shape[0] // own_blocks
    demo_count = demo.shape[0] // blk
    n = lax.axis_size("roll")
    reps = lax.axis_size("rep")
    part = lax.axis_index("rep")
    share = demo_count // reps
    own_demo = lax.dynamic_slice_in_dim(demo, part * (share * blk), share * blk, 0)
    own_v = project(own_demo, projection)
    own_u = project(rollout, projection)
    own_pairs = jnp.concatenate([pair_block, pair_count[:, None]], axis=1)
    own_pairs = jnp.pad(own_pairs, ((0, 0), (0, 128 - own_pairs.shape[1])))
    own = (own_v, norms(own_v, blk), own_u, norms(own_u, blk), own_pairs)
    if n <= DIRECT:
        v, vnorm, u, unorm, pairs = gathered(n, reps, *own)
    else:
        v, vnorm = (lax.all_gather(a, "roll") for a in own[:2])
        u, unorm, pairs = (lax.all_gather(a, "rep") for a in own[2:])
    v, vnorm, u, unorm, pairs = (a.reshape(-1, a.shape[-1]) for a in (v, vnorm, u, unorm, pairs))
    lists = listed(pairs[:, :slots], pairs[:, slots], location, demo_count, share, part)

    roll_pot = jnp.zeros_like(unorm)
    for iteration in range(2):
        sums = run_pass("column", lists, u, v, unorm, vnorm, roll_pot)
        demo_pot = column_potentials(n, sums, iteration)
        kind = "final" if iteration == 1 else "row"
        sums = run_pass(kind, lists, u, v, unorm, vnorm, demo_pot)
        sums = row_totals(reps, sums, iteration)
        heights = sums[0] + FLOOR
        roll_pot = SHIFT - jnp.log2(heights)
    reward = -(sums[1] + UNMATCHED * FLOOR) / heights
    mine = lax.axis_index("roll") * share
    own_pot = lax.all_gather(lax.dynamic_slice_in_dim(demo_pot, mine, share, 0), "rep", tiled=True)
    first = part * own_blocks
    return (
        lax.dynamic_slice_in_dim(reward, first, own_blocks, 0).reshape(-1),
        lax.dynamic_slice_in_dim(roll_pot, first, own_blocks, 0).reshape(-1) / SCALE,
        own_pot.reshape(-1) / SCALE,
    )


def solution(mesh):
    placed = (
        P(("roll", "rep"), None),
        P("roll", None),
        P(),
        P(),
        P(("roll", "rep"), None),
        P(("roll", "rep")),
    )
    return jax.shard_map(
        body,
        mesh=mesh,
        in_specs=placed,
        out_specs=(P(("roll", "rep")), P(("roll", "rep")), P("roll")),
        check_vma=False,
    )
```

```python
import functools
import math

import jax
import jax.numpy as jnp
from jax import lax
from jax.experimental import pallas as pl
from jax.experimental.pallas import tpu as pltpu
from jax.sharding import PartitionSpec as P

ITERS = 2
EPSILON = 0.02
UNMATCHED = 2.0
SLACK = -100.0
LOG2E = math.log2(math.e)
SCALE = LOG2E / EPSILON
SHIFT = 50.0 * LOG2E
FLOOR = math.exp(SLACK + 50.0)
UNROLL = 4
DIRECT = 16
MIB = 1024 * 1024
MESH = pl.DeviceIdType.MESH


def pass_kernel(kind, first, lists_ref, u_ref, v_ref, unorm_ref, vnorm_ref, pot_ref, *rest):
    roll_blocks, blk = unorm_ref.shape
    feats = u_ref.shape[1]
    unit = SCALE / feats
    if kind == "column":
        out_ref, row_term, col_acc = rest
        col_acc[...] = jnp.zeros_like(col_acc)
    elif kind == "row":
        out_ref, row_term, col_term, acc = rest
        acc[...] = jnp.zeros_like(acc)
    else:
        out_ref, row_term, col_term, acc, wacc = rest
        acc[...] = jnp.zeros_like(acc)
        wacc[...] = jnp.zeros_like(wacc)

    def prepare(b, carry):
        line = unorm_ref[pl.ds(b, 1), :] * (-unit)
        if kind == "column":
            line = line + (SHIFT if first else pot_ref[pl.ds(b, 1), :] + SHIFT)
        row_term[pl.ds(b * blk, blk), :] = jnp.transpose(jnp.broadcast_to(line, (blk, blk)))
        return carry

    lax.fori_loop(0, roll_blocks, prepare, 0, unroll=8)
    if kind != "column":
        col_term[...] = pot_ref[...] + SHIFT

    total = lists_ref[2, 0]

    def step(k, carry):
        parts = []
        for p in range(UNROLL):
            at = k * UNROLL + p
            b = lists_ref[0, at]
            t = lists_ref[1, at]
            live = jnp.where(at < total, 0.0, -1e30)
            rows = pl.ds(pl.multiple_of(b * blk, blk), blk)
            crossed = lax.dot_general(
                u_ref[rows, :],
                v_ref[pl.ds(pl.multiple_of(t * blk, blk), blk), :],
                (((1,), (1,)), ((), ())),
                preferred_element_type=jnp.float32,
            )
            y = crossed * (2.0 * unit) + row_term[rows, :]
            line = vnorm_ref[pl.ds(t, 1), :] * (-unit)
            if kind == "column":
                e = jnp.exp2(y + (line + live))
                parts.append((t, jnp.sum(e.reshape(blk // 8, 8, blk), axis=0)))
            elif kind == "row":
                e = jnp.exp2(y + (line + (col_term[pl.ds(t, 1), :] + live)))
                parts.append((rows, e))
            else:
                y = y + line
                e = jnp.exp2(y + (col_term[pl.ds(t, 1), :] + live))
                parts.append((rows, e, e * y))
        for part in parts:
            if kind == "column":
                at8 = pl.ds(pl.multiple_of(part[0] * 8, 8), 8)
                col_acc[at8, :] = col_acc[at8, :] + part[1]
            else:
                acc[part[0], :] = acc[part[0], :] + part[1]
                if kind == "final":
                    wacc[part[0], :] = wacc[part[0], :] + part[2]
        return carry

    lax.fori_loop(0, (total + UNROLL - 1) // UNROLL, step, 0)

    if kind == "column":
        targets = out_ref.shape[0]
        out_ref[...] = jnp.sum(col_acc[...].reshape(targets, 8, blk), axis=1)
    else:

        def finish(b, carry):
            rows = pl.ds(pl.multiple_of(b * blk, blk), blk)
            out_ref[0, pl.ds(b, 1), :] = jnp.sum(jnp.transpose(acc[rows, :]), axis=0, keepdims=True)
            if kind == "final":
                out_ref[1, pl.ds(b, 1), :] = jnp.sum(
                    jnp.transpose(wacc[rows, :]), axis=0, keepdims=True
                ) * (-1.0 / SCALE)
            return carry

        lax.fori_loop(0, roll_blocks, finish, 0, unroll=8)


def run_pass(kind, first, lists, u, v, unorm, vnorm, pot):
    roll_blocks, blk = unorm.shape
    targets = vnorm.shape[0]
    smem = pl.BlockSpec(memory_space=pltpu.SMEM)
    vmem = pl.BlockSpec(memory_space=pltpu.VMEM)
    frames = pltpu.VMEM((roll_blocks * blk, blk), jnp.float32)
    if kind == "column":
        out = jax.ShapeDtypeStruct((targets, blk), jnp.float32)
        scratch = [frames, pltpu.VMEM((targets * 8, blk), jnp.float32)]
    else:
        out = jax.ShapeDtypeStruct((2 if kind == "final" else 1, roll_blocks, blk), jnp.float32)
        scratch = [frames, pltpu.VMEM((targets, blk), jnp.float32), frames]
        if kind == "final":
            scratch.append(frames)
    pairs = lists.shape[1] // 3
    held = sum(math.prod(a.shape) * a.dtype.itemsize for a in [u, v, out] + scratch)
    return pl.pallas_call(
        functools.partial(pass_kernel, kind, first),
        out_shape=out,
        in_specs=[smem] + [vmem] * 5,
        out_specs=vmem,
        scratch_shapes=scratch,
        compiler_params=pltpu.CompilerParams(vmem_limit_bytes=held + 3 * MIB),
        cost_estimate=pl.CostEstimate(
            flops=2 * pairs * blk * blk * u.shape[1],
            bytes_accessed=2 * (u.size + v.size),
            transcendentals=pairs * blk * blk,
        ),
        name="pass_" + kind,
    )(lists, u, v, unorm, vnorm, pot)


def listed(pair_block, pair_count, location, demo_count, share, part):
    roll_blocks, slots = pair_block.shape
    n = roll_blocks * slots
    names = jnp.arange(location.shape[0], dtype=jnp.int32)
    flat = pair_block.reshape(n)
    stored = jnp.sum(jnp.where(flat[:, None] == names[None, :], location[None, :], 0), axis=1)
    active = (jnp.arange(slots, dtype=jnp.int32)[None, :] < pair_count[:, None]).reshape(n)
    local = stored % demo_count
    mine = active & (local // share == part)
    target = (stored // demo_count) * share + local % share
    ids = jnp.arange(n, dtype=jnp.int32)
    rank = jnp.sum((mine[None, :] & (ids[None, :] < ids[:, None])).astype(jnp.int32), axis=1)
    place = jnp.where(mine, rank, -1)
    hit = place[None, :] == ids[:, None]
    home = jnp.sum(jnp.where(hit, (ids // slots)[None, :], 0), axis=1)
    target = jnp.sum(jnp.where(hit, target[None, :], 0), axis=1)
    total = jnp.sum(mine.astype(jnp.int32)).reshape(1)
    lists = jnp.stack([home, target, jnp.broadcast_to(total, (n,))])
    return jnp.pad(lists, ((0, 0), (0, 128)))


def project(frames, projection):
    return jnp.dot(frames, projection, preferred_element_type=jnp.float32).astype(jnp.bfloat16)


def norms(codes, blk):
    wide = codes.astype(jnp.float32)
    return jnp.sum(wide * wide, axis=1).reshape(-1, blk)


def greet(partners):
    barrier = pltpu.get_barrier_semaphore()
    for partner in partners:
        pl.semaphore_signal(barrier, inc=1, device_id=partner, device_id_type=MESH)
    pl.semaphore_wait(barrier, len(partners))


def others(axis, size):
    me = lax.axis_index(axis)
    return [{axis: lax.rem(me + d, size)} for d in range(1, size)]


def block_norms(codes):
    wide = codes.astype(jnp.float32)
    square = wide * wide
    high = square.astype(jnp.bfloat16)
    low = (square - high.astype(jnp.float32)).astype(jnp.bfloat16)
    ones = jnp.ones((8, codes.shape[1]), jnp.bfloat16)
    dims = (((1,), (1,)), ((), ()))
    total = lax.dot_general(ones, high, dims, preferred_element_type=jnp.float32)
    total = total + lax.dot_general(ones, low, dims, preferred_element_type=jnp.float32)
    return total[0:1, :]


def packed_pairs(pairs, location, slots, demo_count, share, part, width):
    blocks = pairs.shape[0]
    names = lax.broadcasted_iota(jnp.int32, (blocks, location.shape[1]), 1)
    places = lax.broadcasted_iota(jnp.int32, (blocks, width), 1).astype(jnp.float32)
    number = lax.broadcasted_iota(jnp.int32, (blocks, width), 0).astype(jnp.float32)
    count = pairs[:, slots : slots + 1]
    where_held = location.astype(jnp.float32)
    mine, target = [], []
    for s in range(slots):
        hit = pairs[:, s : s + 1] == names
        stored = jnp.sum(jnp.where(hit, where_held, 0.0), axis=1, keepdims=True)
        owner = jnp.floor((stored + 0.5) * (1.0 / demo_count))
        local = stored - owner * demo_count
        side = jnp.floor((local + 0.5) * (1.0 / share))
        mine.append(jnp.where((count > s) & (side == part.astype(jnp.float32)), 1.0, 0.0))
        target.append(owner * share + local - side * share)
    in_row = sum(mine)
    below = lax.broadcasted_iota(jnp.int32, (blocks, blocks), 1) < lax.broadcasted_iota(jnp.int32, (blocks, blocks), 0)
    spread = jnp.broadcast_to(in_row, (blocks, 128)).astype(jnp.bfloat16)
    before = jnp.dot(below.astype(jnp.float32).astype(jnp.bfloat16), spread, preferred_element_type=jnp.float32)
    rank = before[:, 0:1]
    homes = jnp.zeros((blocks, width), jnp.float32)
    targets = jnp.zeros((blocks, width), jnp.float32)
    for s in range(slots):
        hit = (rank == places) & (mine[s] > 0.5)
        homes = homes + jnp.where(hit, number, 0.0)
        targets = targets + jnp.where(hit, target[s], 0.0)
        rank = rank + mine[s]
    total = jnp.sum(jnp.broadcast_to(in_row, (blocks, width)), axis=0, keepdims=True)
    rows = [jnp.sum(homes, axis=0, keepdims=True), jnp.sum(targets, axis=0, keepdims=True), total]
    return [row.astype(jnp.int32) for row in rows]


def gather_kernel(n, reps, slots, *refs):
    demo, rollout, projection, own_pairs, location = refs[:5]
    v, vnorm, u, unorm, lists = refs[5:10]
    (demo_in, rollout_in, own_v, own_vnorm, own_u, own_unorm, pairs,
     ring_send, ring_recv, side_send, side_recv, norm_send, norm_recv, rep_send, rep_recv, home) = refs[10:]
    me = lax.axis_index("roll")
    part = lax.axis_index("rep")
    chips = n // 2
    hops = chips // 2
    core = lax.rem(me, 2)
    chip = me // 2
    odd = lax.rem(chip, 2)
    place = (1 - odd) * (chip // 2) + odd * (chips - 1 - chip // 2)

    def at_place(p):
        p = lax.rem(p + 2 * chips, chips)
        high = p // hops
        return ((1 - high) * (2 * p) + high * (2 * (chips - 1 - p) + 1)) * 2 + core

    twin = {"roll": me + 1 - 2 * core}
    ways = ({"roll": at_place(place + 1)}, {"roll": at_place(place - 1)})
    rows = own_v.shape[0] // 2
    share, blk = own_vnorm.shape
    own_blocks = own_unorm.shape[0]
    near = others("roll", n) + others("rep", reps)
    fetch_demo = pltpu.make_async_copy(demo.at[pl.ds(part * (share * blk), share * blk)], demo_in, home.at[4])
    fetch_demo.start()
    fetch_rollout = pltpu.make_async_copy(rollout, rollout_in, home.at[5])
    fetch_rollout.start()
    barrier = pltpu.get_barrier_semaphore()
    for partner in near:
        pl.semaphore_signal(barrier, inc=1, device_id=partner, device_id_type=MESH)
    fetch_demo.wait()
    for half in range(2):
        piece = pl.ds(half * rows, rows)
        own_v[piece, :] = jnp.dot(
            demo_in[piece, :], projection[...], preferred_element_type=jnp.float32
        ).astype(jnp.bfloat16)
    pl.semaphore_wait(barrier, len(near))

    waits = []

    def origin(way, s):
        return at_place(place - s) if way == 0 else at_place(place + s)

    def chunk(s, way, half):
        piece = pl.ds(half * rows, rows)
        if s == 0:
            return own_v.at[piece], v.at[me, piece]
        block = origin(way, s)
        return v.at[block, piece], v.at[block, piece]

    def send(s, way, half):
        source, target = chunk(s, way, half)
        copy = pltpu.make_async_remote_copy(
            src_ref=source, dst_ref=target,
            send_sem=ring_send.at[way, s, half], recv_sem=ring_recv.at[way, s, half],
            device_id=ways[way], device_id_type=MESH,
        )
        copy.start()
        return copy

    def cross(s, way, half):
        source, target = chunk(s, way, half)
        copy = pltpu.make_async_remote_copy(
            src_ref=source, dst_ref=target,
            send_sem=side_send.at[way, s, half], recv_sem=side_recv.at[way, s, half],
            device_id=twin, device_id_type=MESH,
        )
        copy.start()
        waits.append(copy)

    def travels(s, way, half):
        return s < hops - 1 or (s == hops - 1 and half == way)

    moving = {}
    for half in range(2):
        for way in range(2):
            if travels(0, way, half):
                moving[0, way, half] = send(0, way, half)

    def spread(source, target, axis, which, sends, recvs):
        started = []
        for d, partner in enumerate(others(axis, reps if axis == "rep" else n)):
            copy = pltpu.make_async_remote_copy(
                src_ref=source, dst_ref=target,
                send_sem=sends.at[which, d], recv_sem=recvs.at[which, d],
                device_id=partner, device_id_type=MESH,
            )
            copy.start()
            started.append(copy)
        return started

    pair_copies = spread(own_pairs, pairs.at[part], "rep", 0, rep_send, rep_recv)
    pairs[part] = own_pairs[...]
    for half in range(2):
        cross(0, 0, half)
    fetch_rollout.wait()

    def do_rollout(b, carry):
        rows_b = pl.ds(pl.multiple_of(b * blk, blk), blk)
        codes = jnp.dot(
            rollout_in[rows_b, :], projection[...], preferred_element_type=jnp.float32
        ).astype(jnp.bfloat16)
        own_u[rows_b, :] = codes
        own_unorm[pl.ds(b, 1), :] = block_norms(codes)
        return carry

    lax.fori_loop(0, own_blocks, do_rollout, 0)
    waits += spread(own_u, u.at[part], "rep", 1, rep_send, rep_recv)
    waits += spread(own_unorm, unorm.at[part], "rep", 2, rep_send, rep_recv)

    def do_demo(b, carry):
        own_vnorm[pl.ds(b, 1), :] = block_norms(own_v[pl.ds(pl.multiple_of(b * blk, blk), blk), :])
        return carry

    lax.fori_loop(0, share, do_demo, 0)
    waits += spread(own_vnorm, vnorm.at[me], "roll", 0, norm_send, norm_recv)
    stays = []
    for k, (source, target) in enumerate(
        ((own_v, v.at[me]), (own_vnorm, vnorm.at[me]), (own_u, u.at[part]), (own_unorm, unorm.at[part]))
    ):
        copy = pltpu.make_async_copy(source, target, home.at[k])
        copy.start()
        stays.append(copy)
    for copy in pair_copies:
        copy.wait()
    everyone = pairs[...].reshape(reps * own_blocks, pairs.shape[2])
    found = packed_pairs(everyone, location[...], slots, share * reps, share, part, lists.shape[1])
    lists[...] = jnp.zeros_like(lists)
    for k, row in enumerate(found):
        lists[k : k + 1, :] = row
    for s in range(1, hops + 1):
        for half in range(2):
            for way in range(2):
                if (s - 1, way, half) not in moving:
                    continue
                moving[s - 1, way, half].wait_recv()
                if travels(s, way, half):
                    moving[s, way, half] = send(s, way, half)
                cross(s, way, half)
    for copy in moving.values():
        copy.wait_send()
    for copy in stays:
        copy.wait()
    for copy in waits:
        copy.wait()


def gathered(n, reps, demo, rollout, projection, pair_block, pair_count, location):
    hops = n // 4
    own_blocks, slots = pair_block.shape
    blk = rollout.shape[0] // own_blocks
    feats = projection.shape[1]
    share = demo.shape[0] // blk // reps
    own_pairs = jnp.concatenate([pair_block, pair_count[:, None]], axis=1)
    own_pairs = jnp.pad(own_pairs, ((0, 0), (0, 128 - own_pairs.shape[1])))
    anywhere = pl.BlockSpec(memory_space=pl.ANY)
    vmem = pl.BlockSpec(memory_space=pltpu.VMEM)
    dma = pltpu.SemaphoreType.DMA
    wide, code = jnp.float32, jnp.bfloat16
    return pl.pallas_call(
        functools.partial(gather_kernel, n, reps, slots),
        out_shape=[
            jax.ShapeDtypeStruct((n, share * blk, feats), code),
            jax.ShapeDtypeStruct((n, share, blk), wide),
            jax.ShapeDtypeStruct((reps, own_blocks * blk, feats), code),
            jax.ShapeDtypeStruct((reps, own_blocks, blk), wide),
            jax.ShapeDtypeStruct((8, reps * own_blocks * slots + 128), jnp.int32),
        ],
        in_specs=[anywhere, anywhere, vmem, vmem, vmem],
        out_specs=[anywhere] * 4 + [vmem],
        scratch_shapes=[
            pltpu.VMEM((share * blk, feats), code),
            pltpu.VMEM(rollout.shape, code),
            pltpu.VMEM((share * blk, feats), code),
            pltpu.VMEM((share, blk), wide),
            pltpu.VMEM((own_blocks * blk, feats), code),
            pltpu.VMEM((own_blocks, blk), wide),
            pltpu.VMEM((reps,) + own_pairs.shape, jnp.int32),
            dma((2, hops, 2)), dma((2, hops, 2)),
            dma((2, hops + 1, 2)), dma((2, hops + 1, 2)),
            dma((1, n - 1)), dma((1, n - 1)),
            dma((3, reps - 1)), dma((3, reps - 1)),
            dma((6,)),
        ],
        compiler_params=pltpu.CompilerParams(
            collective_id=0, has_side_effects=True, vmem_limit_bytes=8 * MIB
        ),
        name="gather_codes",
    )(demo, rollout, projection, own_pairs, location[None, :])


def column_kernel(n, reps, sums, *refs):
    if reps:
        out, both, landed, full, held, first_send, first_recv, second_send, second_recv, rep_send, rep_recv = refs
    else:
        out, landed, full, first_send, first_recv, second_send, second_recv = refs
    me = lax.axis_index("roll")
    partners = others("roll", n)
    twins = others("rep", reps) if reps else []
    greet(partners + twins)
    copies = []
    for d, partner in enumerate(partners):
        copy = pltpu.make_async_remote_copy(
            src_ref=sums.at[partner["roll"]], dst_ref=landed.at[d],
            send_sem=first_send.at[d], recv_sem=first_recv.at[d],
            device_id=partner, device_id_type=MESH,
        )
        copy.start()
        copies.append(copy)
    total = sums[me]
    for d, copy in enumerate(copies):
        copy.wait_recv()
        total = total + landed[d]
    pot = SHIFT - jnp.log2(total + FLOOR)
    full[me] = pot
    seconds = []
    for d, partner in enumerate(partners):
        copy = pltpu.make_async_remote_copy(
            src_ref=full.at[me], dst_ref=full.at[me],
            send_sem=second_send.at[d], recv_sem=second_recv.at[d],
            device_id=partner, device_id_type=MESH,
        )
        copy.start()
        seconds.append(copy)
    if reps:
        part = lax.axis_index("rep")
        held[part] = pot * (1.0 / SCALE)
        for d, partner in enumerate(twins):
            copy = pltpu.make_async_remote_copy(
                src_ref=held.at[part], dst_ref=held.at[part],
                send_sem=rep_send.at[d], recv_sem=rep_recv.at[d],
                device_id=partner, device_id_type=MESH,
            )
            copy.start()
            seconds.append(copy)
    for copy in copies:
        copy.wait_send()
    for copy in seconds:
        copy.wait()
    out[...] = full[...]
    if reps:
        both[...] = held[...]


def column_potentials(n, reps, sums, call):
    last = call == ITERS - 1
    share, blk = sums.shape[0] // n, sums.shape[1]
    if n > DIRECT:
        pot = SHIFT - jnp.log2(lax.psum(sums, "roll") + FLOOR)
        if not last:
            return pot, None
        mine = lax.dynamic_slice_in_dim(pot, lax.axis_index("roll") * share, share, 0)
        return pot, lax.all_gather(mine, "rep") / SCALE
    sums = sums.reshape(n, share, blk)
    dma = pltpu.SemaphoreType.DMA
    vmem = pl.BlockSpec(memory_space=pltpu.VMEM)
    both = (reps, share, blk)
    outs = [jax.ShapeDtypeStruct(sums.shape, sums.dtype)]
    scratch = [pltpu.VMEM((n - 1, share, blk), jnp.float32), pltpu.VMEM((n, share, blk), jnp.float32)]
    if last:
        outs.append(jax.ShapeDtypeStruct(both, sums.dtype))
        scratch.append(pltpu.VMEM(both, jnp.float32))
    scratch += [dma((n - 1,))] * 4
    if last:
        scratch += [dma((reps - 1,))] * 2
    out = pl.pallas_call(
        functools.partial(column_kernel, n, reps if last else 0),
        out_shape=outs,
        in_specs=[vmem],
        out_specs=[vmem] * len(outs),
        scratch_shapes=scratch,
        compiler_params=pltpu.CompilerParams(
            collective_id=1 + call, has_side_effects=True, vmem_limit_bytes=MIB
        ),
        name="column_exchange_%d" % call,
    )(sums)
    return out[0].reshape(n * share, blk), out[1] if last else None


def row_kernel(reps, last, sums, *refs):
    outs, (landed, send_sem, recv_sem) = refs[:-3], refs[-3:]
    part = lax.axis_index("rep")
    partners = others("rep", reps)
    greet(partners)
    copies = []
    for d, partner in enumerate(partners):
        copy = pltpu.make_async_remote_copy(
            src_ref=sums, dst_ref=landed.at[d], send_sem=send_sem.at[d], recv_sem=recv_sem.at[d],
            device_id=partner, device_id_type=MESH,
        )
        copy.start()
        copies.append(copy)
    for copy in copies:
        copy.wait_recv()
    if last:
        heights, weighted = (
            sum((landed[d, k, part] for d in range(reps - 1)), sums[k, part]) for k in range(2)
        )
        heights = heights + FLOOR
        outs[0][...] = -(weighted + UNMATCHED * FLOOR) / heights
        outs[1][...] = (SHIFT - jnp.log2(heights)) * (1.0 / SCALE)
    else:
        total = sum((landed[d, 0] for d in range(reps - 1)), sums[0])
        outs[0][...] = SHIFT - jnp.log2(total + FLOOR)
    for copy in copies:
        copy.wait_send()


def row_totals(reps, sums, call):
    last = call == ITERS - 1
    sums = sums.reshape(sums.shape[0], reps, -1, sums.shape[2])
    dma = pltpu.SemaphoreType.DMA((reps - 1,))
    vmem = pl.BlockSpec(memory_space=pltpu.VMEM)
    shapes = [sums.shape[2:]] * 2 if last else [sums.shape[1:]]
    return pl.pallas_call(
        functools.partial(row_kernel, reps, last),
        out_shape=[jax.ShapeDtypeStruct(shape, sums.dtype) for shape in shapes],
        in_specs=[vmem],
        out_specs=[vmem] * len(shapes),
        scratch_shapes=[pltpu.VMEM((reps - 1,) + sums.shape, jnp.float32), dma, dma],
        compiler_params=pltpu.CompilerParams(
            collective_id=1 + ITERS + call, has_side_effects=True, vmem_limit_bytes=2 * MIB
        ),
        name="row_exchange_%d" % call,
    )(sums)


def body(rollout, demo, projection, location, pair_block, pair_count):
    blk = rollout.shape[0] // pair_block.shape[0]
    n = lax.axis_size("roll")
    reps = lax.axis_size("rep")
    if n <= DIRECT:
        v, vnorm, u, unorm, lists = gathered(
            n, reps, demo, rollout, projection, pair_block, pair_count, location
        )
    else:
        part = lax.axis_index("rep")
        demo_count = demo.shape[0] // blk
        share = demo_count // reps
        own_demo = lax.dynamic_slice_in_dim(demo, part * (share * blk), share * blk, 0)
        own_v = project(own_demo, projection)
        own_u = project(rollout, projection)
        v, vnorm = (lax.all_gather(a, "roll") for a in (own_v, norms(own_v, blk)))
        u, unorm = (lax.all_gather(a, "rep") for a in (own_u, norms(own_u, blk)))
        pairs, counts = (lax.all_gather(a, "rep", tiled=True) for a in (pair_block, pair_count))
        lists = listed(pairs, counts, location, demo_count, share, part)
    v, vnorm, u, unorm = (a.reshape(-1, a.shape[-1]) for a in (v, vnorm, u, unorm))

    roll_pot = unorm
    for iteration in range(ITERS):
        sums = run_pass("column", iteration == 0, lists, u, v, unorm, vnorm, roll_pot)
        demo_pot, held_pot = column_potentials(n, reps, sums, iteration)
        kind = "final" if iteration == ITERS - 1 else "row"
        sums = run_pass(kind, False, lists, u, v, unorm, vnorm, demo_pot)
        results = row_totals(reps, sums, iteration)
        roll_pot = results[0].reshape(unorm.shape) if kind == "row" else None
    return results[0].reshape(-1), results[1].reshape(-1), held_pot.reshape(-1)


def solution(mesh):
    placed = (
        P(("roll", "rep"), None),
        P("roll", None),
        P(),
        P(),
        P(("roll", "rep"), None),
        P(("roll", "rep")),
    )
    return jax.shard_map(
        body,
        mesh=mesh,
        in_specs=placed,
        out_specs=(P(("roll", "rep")), P(("roll", "rep")), P("roll")),
        check_vma=False,
    )
```

```python
import functools
import math

import jax
import jax.numpy as jnp
from jax import lax
from jax.experimental import pallas as pl
from jax.experimental.pallas import tpu as pltpu
from jax.sharding import PartitionSpec as P

ITERS = 2
EPSILON = 0.02
UNMATCHED = 2.0
SLACK = -100.0
LOG2E = math.log2(math.e)
SCALE = LOG2E / EPSILON
SHIFT = 50.0 * LOG2E
FLOOR = math.exp(SLACK + 50.0)
UNROLL = 4
DIRECT = 16
MIB = 1024 * 1024
MESH = pl.DeviceIdType.MESH


def pass_kernel(kind, fresh, stored, lists_ref, *refs):
    refs = list(refs)
    reads = stored and not fresh
    if reads:
        kept = refs.pop(0)
    else:
        u_ref, v_ref, unorm_ref, vnorm_ref = refs[:4]
        refs = refs[4:]
    pot_ref = None if fresh else refs.pop(0)
    out_ref = refs.pop(0)
    if stored and fresh:
        kept = refs.pop(0)
    sums_ref = refs.pop()
    if kind == "final":
        wsums_ref = refs.pop()
        wsums_ref[...] = jnp.zeros_like(wsums_ref)
    sums_ref[...] = jnp.zeros_like(sums_ref)
    blk = out_ref.shape[-1]
    by_column = kind == "column"
    roll_blocks = (refs[0] if refs else sums_ref).shape[0] // blk

    if not reads:
        row_norm = refs.pop(0)
        unit = SCALE / u_ref.shape[1]
        roll_blocks = unorm_ref.shape[0]

    def spread(source, factor, target):
        def one(b, carry):
            line = source[pl.ds(b, 1), :] * factor
            rows = pl.ds(pl.multiple_of(b * blk, blk), blk)
            target[rows, :] = jnp.transpose(jnp.broadcast_to(line, (blk, blk)))
            return carry

        lax.fori_loop(0, roll_blocks, one, 0, unroll=8)

    if not reads:
        spread(unorm_ref, -unit, row_norm)
    if by_column and not fresh:
        row_pot = refs.pop(0)
        spread(pot_ref, 1.0, row_pot)

    total = lists_ref[2, 0]

    def step(k, carry):
        parts = []
        for p in range(UNROLL):
            at = k * UNROLL + p
            b = lists_ref[0, at]
            t = lists_ref[1, at]
            live = jnp.where(at < total, SHIFT, -1e30)
            rows = pl.ds(pl.multiple_of(b * blk, blk), blk)
            here = pl.ds(pl.multiple_of(at * blk, blk), blk)
            if reads:
                y = kept[here, :]
            else:
                crossed = lax.dot_general(
                    u_ref[rows, :],
                    v_ref[pl.ds(pl.multiple_of(t * blk, blk), blk), :],
                    (((1,), (1,)), ((), ())),
                    preferred_element_type=jnp.float32,
                )
                y = crossed * (2.0 * unit) + row_norm[rows, :] + vnorm_ref[pl.ds(t, 1), :] * (-unit)
                if stored:
                    kept[here, :] = y
            if by_column:
                x = y + live if fresh else y + row_pot[rows, :] + live
                parts.append((t, jnp.sum(jnp.exp2(x).reshape(blk // 8, 8, blk), axis=0)))
            else:
                e = jnp.exp2(y + (pot_ref[pl.ds(t, 1), :] + live))
                parts.append((rows, e, e * y if kind == "final" else None))
        for where, e, *weighted in parts:
            if by_column:
                at8 = pl.ds(pl.multiple_of(where * 8, 8), 8)
                sums_ref[at8, :] = sums_ref[at8, :] + e
            else:
                sums_ref[where, :] = sums_ref[where, :] + e
                if kind == "final":
                    wsums_ref[where, :] = wsums_ref[where, :] + weighted[0]
        return carry

    lax.fori_loop(0, (total + UNROLL - 1) // UNROLL, step, 0)

    if by_column:
        out_ref[...] = jnp.sum(sums_ref[...].reshape(out_ref.shape[0], 8, blk), axis=1)
    else:

        def finish(b, carry):
            rows = pl.ds(pl.multiple_of(b * blk, blk), blk)
            out_ref[0, pl.ds(b, 1), :] = jnp.sum(jnp.transpose(sums_ref[rows, :]), axis=0, keepdims=True)
            if kind == "final":
                out_ref[1, pl.ds(b, 1), :] = jnp.sum(
                    jnp.transpose(wsums_ref[rows, :]), axis=0, keepdims=True
                ) * (-1.0 / SCALE)
            return carry

        lax.fori_loop(0, roll_blocks, finish, 0, unroll=8)


def run_pass(kind, lists, u, v, unorm, vnorm, pot, kept, stored):
    fresh = pot is None
    roll_blocks, blk = unorm.shape
    targets = vnorm.shape[0]
    pairs = lists.shape[1] - 128
    smem = pl.BlockSpec(memory_space=pltpu.SMEM)
    vmem = pl.BlockSpec(memory_space=pltpu.VMEM)
    frames = pltpu.VMEM((roll_blocks * blk, blk), jnp.float32)
    by_column = kind == "column"
    reads = stored and not fresh
    args = [kept] if reads else [u, v, unorm, vnorm]
    if not fresh:
        args.append(pot)
    if by_column:
        outs = [jax.ShapeDtypeStruct((targets, blk), jnp.float32)]
        sums = [pltpu.VMEM((targets * 8, blk), jnp.float32)]
    else:
        outs = [jax.ShapeDtypeStruct((2 if kind == "final" else 1, roll_blocks, blk), jnp.float32)]
        sums = [frames] * (2 if kind == "final" else 1)
    if stored and fresh:
        outs.append(jax.ShapeDtypeStruct(((pairs + UNROLL) * blk, blk), jnp.float32))
    scratch = ([] if reads else [frames]) + ([frames] if by_column and not fresh else []) + sums
    held = sum(math.prod(a.shape) * a.dtype.itemsize for a in scratch + ([] if stored else args + outs))
    return pl.pallas_call(
        functools.partial(pass_kernel, kind, fresh, stored),
        out_shape=outs,
        in_specs=[smem] + [vmem] * len(args),
        out_specs=[vmem] * len(outs),
        scratch_shapes=scratch,
        compiler_params=pltpu.CompilerParams(vmem_limit_bytes=held + 2 * MIB),
        cost_estimate=pl.CostEstimate(
            flops=0 if reads else pairs * blk * blk * u.shape[1],
            bytes_accessed=2 * v.size,
            transcendentals=pairs * blk * blk // 2,
        ),
        name="pass_" + kind,
    )(lists, *args)


def listed(pair_block, pair_count, location, demo_count, share, part):
    roll_blocks, slots = pair_block.shape
    n = roll_blocks * slots
    names = jnp.arange(location.shape[0], dtype=jnp.int32)
    flat = pair_block.reshape(n)
    stored = jnp.sum(jnp.where(flat[:, None] == names[None, :], location[None, :], 0), axis=1)
    active = (jnp.arange(slots, dtype=jnp.int32)[None, :] < pair_count[:, None]).reshape(n)
    local = stored % demo_count
    mine = active & (local // share == part)
    target = (stored // demo_count) * share + local % share
    ids = jnp.arange(n, dtype=jnp.int32)
    rank = jnp.sum((mine[None, :] & (ids[None, :] < ids[:, None])).astype(jnp.int32), axis=1)
    place = jnp.where(mine, rank, -1)
    hit = place[None, :] == ids[:, None]
    home = jnp.sum(jnp.where(hit, (ids // slots)[None, :], 0), axis=1)
    target = jnp.sum(jnp.where(hit, target[None, :], 0), axis=1)
    total = jnp.sum(mine.astype(jnp.int32)).reshape(1)
    lists = jnp.stack([home, target, jnp.broadcast_to(total, (n,))])
    return jnp.pad(lists, ((0, 0), (0, 128)))


def project(frames, projection):
    return jnp.dot(frames, projection, preferred_element_type=jnp.float32).astype(jnp.bfloat16)


def norms(codes, blk):
    wide = codes.astype(jnp.float32)
    return jnp.sum(wide * wide, axis=1).reshape(-1, blk)


def greet(partners):
    barrier = pltpu.get_barrier_semaphore()
    for partner in partners:
        pl.semaphore_signal(barrier, inc=1, device_id=partner, device_id_type=MESH)
    pl.semaphore_wait(barrier, len(partners))


def others(axis, size):
    me = lax.axis_index(axis)
    return [{axis: lax.rem(me + d, size)} for d in range(1, size)]


def block_norms(codes):
    wide = codes.astype(jnp.float32)
    square = wide * wide
    high = square.astype(jnp.bfloat16)
    low = (square - high.astype(jnp.float32)).astype(jnp.bfloat16)
    ones = jnp.ones((8, codes.shape[1]), jnp.bfloat16)
    dims = (((1,), (1,)), ((), ()))
    total = lax.dot_general(ones, high, dims, preferred_element_type=jnp.float32)
    total = total + lax.dot_general(ones, low, dims, preferred_element_type=jnp.float32)
    return total[0:1, :]


def packed_pairs(pairs, location, slots, demo_count, share, part, width):
    blocks = pairs.shape[0]
    names = lax.broadcasted_iota(jnp.int32, (blocks, 128), 1).astype(jnp.float32)
    places = lax.broadcasted_iota(jnp.int32, (blocks, width), 1).astype(jnp.float32)
    number = lax.broadcasted_iota(jnp.int32, (blocks, width), 0).astype(jnp.float32)
    count = pairs[:, slots : slots + 1]
    where_held = location.astype(jnp.float32)
    mine, target = [], []
    for s in range(slots):
        found = jnp.zeros((blocks, 128), jnp.float32)
        for k in range(location.shape[0]):
            hit = pairs[:, s : s + 1] - 128.0 * k == names
            found = found + jnp.where(hit, where_held[k : k + 1, :], 0.0)
        stored = jnp.sum(found, axis=1, keepdims=True)
        owner = jnp.floor((stored + 0.5) * (1.0 / demo_count))
        local = stored - owner * demo_count
        side = jnp.floor((local + 0.5) * (1.0 / share))
        mine.append(jnp.where((count > s) & (side == part.astype(jnp.float32)), 1.0, 0.0))
        target.append(owner * share + local - side * share)
    in_row = sum(mine)
    below = lax.broadcasted_iota(jnp.int32, (blocks, blocks), 1) < lax.broadcasted_iota(jnp.int32, (blocks, blocks), 0)
    spread = jnp.broadcast_to(in_row, (blocks, 128)).astype(jnp.bfloat16)
    before = jnp.dot(below.astype(jnp.float32).astype(jnp.bfloat16), spread, preferred_element_type=jnp.float32)
    rank = before[:, 0:1]
    homes = jnp.zeros((blocks, width), jnp.float32)
    targets = jnp.zeros((blocks, width), jnp.float32)
    for s in range(slots):
        hit = (rank == places) & (mine[s] > 0.5)
        homes = homes + jnp.where(hit, number, 0.0)
        targets = targets + jnp.where(hit, target[s], 0.0)
        rank = rank + mine[s]
    total = jnp.sum(jnp.broadcast_to(in_row, (blocks, width)), axis=0, keepdims=True)
    rows = [jnp.sum(homes, axis=0, keepdims=True), jnp.sum(targets, axis=0, keepdims=True), total]
    return [row.astype(jnp.int32) for row in rows]


def gather_kernel(n, reps, slots, *refs):
    demo, rollout, projection_hbm, pair_block, pair_count, location_hbm = refs[:6]
    v, vnorm, u, unorm, lists = refs[6:11]
    (demo_in, rollout_in, projection, location, block_in, count_in, own_pairs, own_v, own_vnorm, own_u, own_unorm, pairs,
     ring_send, ring_recv, side_send, side_recv, norm_send, norm_recv, rep_send, rep_recv, home) = refs[11:]
    me = lax.axis_index("roll")
    part = lax.axis_index("rep")
    chips = n // 2
    hops = chips // 2
    core = lax.rem(me, 2)
    chip = me // 2
    odd = lax.rem(chip, 2)
    place = (1 - odd) * (chip // 2) + odd * (chips - 1 - chip // 2)

    def at_place(p):
        p = lax.rem(p + 2 * chips, chips)
        high = p // hops
        return ((1 - high) * (2 * p) + high * (2 * (chips - 1 - p) + 1)) * 2 + core

    twin = {"roll": me + 1 - 2 * core}
    ways = ({"roll": at_place(place + 1)}, {"roll": at_place(place - 1)})
    rows = own_v.shape[0] // 2
    share, blk = own_vnorm.shape
    own_blocks = own_unorm.shape[0]
    near = others("roll", n) + others("rep", reps)
    fetch_demo = pltpu.make_async_copy(demo.at[pl.ds(part * (share * blk), share * blk)], demo_in, home.at[4])
    fetch_demo.start()
    fetches = [
        pltpu.make_async_copy(source, target, home.at[6 + k])
        for k, (source, target) in enumerate((
            (projection_hbm, projection),
            (pair_block, block_in),
            (pair_count, count_in),
            (location_hbm, location),
        ))
    ]
    for fetch in fetches:
        fetch.start()
    fetch_rollout = pltpu.make_async_copy(rollout, rollout_in, home.at[5])
    fetch_rollout.start()
    barrier = pltpu.get_barrier_semaphore()
    for partner in near:
        pl.semaphore_signal(barrier, inc=1, device_id=partner, device_id_type=MESH)
    fetch_demo.wait()
    for fetch in fetches:
        fetch.wait()
    own_pairs[...] = jnp.zeros_like(own_pairs)
    own_pairs[0:slots, 0 : block_in.shape[1]] = block_in[...]
    own_pairs[slots : slots + 1, 0 : count_in.shape[1]] = count_in[...]
    for half in range(2):
        piece = pl.ds(half * rows, rows)
        own_v[piece, :] = jnp.dot(
            demo_in[piece, :], projection[...], preferred_element_type=jnp.float32
        ).astype(jnp.bfloat16)
    pl.semaphore_wait(barrier, len(near))

    waits = []

    def origin(way, s):
        return at_place(place - s) if way == 0 else at_place(place + s)

    def chunk(s, way, half):
        piece = pl.ds(half * rows, rows)
        if s == 0:
            return own_v.at[piece], v.at[me, piece]
        block = origin(way, s)
        return v.at[block, piece], v.at[block, piece]

    def send(s, way, half):
        source, target = chunk(s, way, half)
        copy = pltpu.make_async_remote_copy(
            src_ref=source, dst_ref=target,
            send_sem=ring_send.at[way, s, half], recv_sem=ring_recv.at[way, s, half],
            device_id=ways[way], device_id_type=MESH,
        )
        copy.start()
        return copy

    def cross(s, way, half):
        source, target = chunk(s, way, half)
        copy = pltpu.make_async_remote_copy(
            src_ref=source, dst_ref=target,
            send_sem=side_send.at[way, s, half], recv_sem=side_recv.at[way, s, half],
            device_id=twin, device_id_type=MESH,
        )
        copy.start()
        waits.append(copy)

    def travels(s, way, half):
        return s < hops - 1 or (s == hops - 1 and half == way)

    moving = {}
    for half in range(2):
        for way in range(2):
            if travels(0, way, half):
                moving[0, way, half] = send(0, way, half)

    def spread(source, target, axis, which, sends, recvs):
        started = []
        for d, partner in enumerate(others(axis, reps if axis == "rep" else n)):
            copy = pltpu.make_async_remote_copy(
                src_ref=source, dst_ref=target,
                send_sem=sends.at[which, d], recv_sem=recvs.at[which, d],
                device_id=partner, device_id_type=MESH,
            )
            copy.start()
            started.append(copy)
        return started

    pair_copies = spread(own_pairs, pairs.at[part], "rep", 0, rep_send, rep_recv)
    pairs[part] = own_pairs[...]
    for half in range(2):
        cross(0, 0, half)
    fetch_rollout.wait()

    def do_rollout(b, carry):
        rows_b = pl.ds(pl.multiple_of(b * blk, blk), blk)
        codes = jnp.dot(
            rollout_in[rows_b, :], projection[...], preferred_element_type=jnp.float32
        ).astype(jnp.bfloat16)
        own_u[rows_b, :] = codes
        own_unorm[pl.ds(b, 1), :] = block_norms(codes)
        return carry

    lax.fori_loop(0, own_blocks, do_rollout, 0)
    waits += spread(own_u, u.at[part], "rep", 1, rep_send, rep_recv)
    waits += spread(own_unorm, unorm.at[part], "rep", 2, rep_send, rep_recv)

    def do_demo(b, carry):
        own_vnorm[pl.ds(b, 1), :] = block_norms(own_v[pl.ds(pl.multiple_of(b * blk, blk), blk), :])
        return carry

    lax.fori_loop(0, share, do_demo, 0)
    waits += spread(own_vnorm, vnorm.at[me], "roll", 0, norm_send, norm_recv)
    stays = []
    for k, (source, target) in enumerate(
        ((own_v, v.at[me]), (own_vnorm, vnorm.at[me]), (own_u, u.at[part]), (own_unorm, unorm.at[part]))
    ):
        copy = pltpu.make_async_copy(source, target, home.at[k])
        copy.start()
        stays.append(copy)
    for copy in pair_copies:
        copy.wait()
    square = [
        jnp.concatenate([pairs[r].astype(jnp.float32), jnp.zeros((128 - pairs.shape[1], 128), jnp.float32)], axis=0)
        for r in range(reps)
    ]
    everyone = jnp.concatenate([jnp.transpose(a)[0:own_blocks, :] for a in square], axis=0)
    found = packed_pairs(everyone, location[...], slots, share * reps, share, part, lists.shape[1])
    lists[...] = jnp.zeros_like(lists)
    for k, row in enumerate(found):
        lists[k : k + 1, :] = row
    for s in range(1, hops + 1):
        for half in range(2):
            for way in range(2):
                if (s - 1, way, half) not in moving:
                    continue
                moving[s - 1, way, half].wait_recv()
                if travels(s, way, half):
                    moving[s, way, half] = send(s, way, half)
                cross(s, way, half)
    for copy in moving.values():
        copy.wait_send()
    for copy in stays:
        copy.wait()
    for copy in waits:
        copy.wait()


def gathered(n, reps, demo, rollout, projection, pair_block, pair_count, location):
    hops = n // 4
    own_blocks, slots = pair_block.shape
    blk = rollout.shape[0] // own_blocks
    feats = projection.shape[1]
    share = demo.shape[0] // blk // reps
    location = location.reshape(-1, 128)
    own_pairs = (slots // 8 * 8 + 8, 128)
    hbm = pl.BlockSpec(memory_space=pltpu.HBM)
    anywhere = pl.BlockSpec(memory_space=pl.ANY)
    vmem = pl.BlockSpec(memory_space=pltpu.VMEM)
    dma = pltpu.SemaphoreType.DMA
    wide, code = jnp.float32, jnp.bfloat16
    return pl.pallas_call(
        functools.partial(gather_kernel, n, reps, slots),
        out_shape=[
            jax.ShapeDtypeStruct((n, share * blk, feats), code),
            jax.ShapeDtypeStruct((n, share, blk), wide),
            jax.ShapeDtypeStruct((reps, own_blocks * blk, feats), code),
            jax.ShapeDtypeStruct((reps, own_blocks, blk), wide),
            jax.ShapeDtypeStruct((8, reps * own_blocks * slots + 128), jnp.int32),
        ],
        in_specs=[hbm] * 6,
        out_specs=[anywhere] * 4 + [vmem],
        scratch_shapes=[
            pltpu.VMEM((share * blk, feats), code),
            pltpu.VMEM(rollout.shape, code),
            pltpu.VMEM(projection.shape, code),
            pltpu.VMEM(location.shape, jnp.int32),
            pltpu.VMEM((slots, own_blocks), jnp.int32),
            pltpu.VMEM((1, own_blocks), jnp.int32),
            pltpu.VMEM(own_pairs, jnp.int32),
            pltpu.VMEM((share * blk, feats), code),
            pltpu.VMEM((share, blk), wide),
            pltpu.VMEM((own_blocks * blk, feats), code),
            pltpu.VMEM((own_blocks, blk), wide),
            pltpu.VMEM((reps,) + own_pairs, jnp.int32),
            dma((2, hops, 2)), dma((2, hops, 2)),
            dma((2, hops + 1, 2)), dma((2, hops + 1, 2)),
            dma((1, n - 1)), dma((1, n - 1)),
            dma((3, reps - 1)), dma((3, reps - 1)),
            dma((10,)),
        ],
        compiler_params=pltpu.CompilerParams(
            collective_id=0, has_side_effects=True, vmem_limit_bytes=8 * MIB
        ),
        name="gather_codes",
    )(*(
        pltpu.with_memory_space_constraint(a, pltpu.HBM)
        for a in (demo, rollout, projection, pair_block.T, pair_count[None, :], location)
    ))


def column_kernel(n, reps, sums, *refs):
    if reps:
        out, both, landed, full, held, first_send, first_recv, second_send, second_recv, rep_send, rep_recv = refs
    else:
        out, landed, full, first_send, first_recv, second_send, second_recv = refs
    me = lax.axis_index("roll")
    partners = others("roll", n)
    twins = others("rep", reps) if reps else []
    greet(partners + twins)
    copies = []
    for d, partner in enumerate(partners):
        copy = pltpu.make_async_remote_copy(
            src_ref=sums.at[partner["roll"]], dst_ref=landed.at[d],
            send_sem=first_send.at[d], recv_sem=first_recv.at[d],
            device_id=partner, device_id_type=MESH,
        )
        copy.start()
        copies.append(copy)
    total = sums[me]
    for d, copy in enumerate(copies):
        copy.wait_recv()
        total = total + landed[d]
    pot = SHIFT - jnp.log2(total + FLOOR)
    full[me] = pot
    seconds = []
    for d, partner in enumerate(partners):
        copy = pltpu.make_async_remote_copy(
            src_ref=full.at[me], dst_ref=full.at[me],
            send_sem=second_send.at[d], recv_sem=second_recv.at[d],
            device_id=partner, device_id_type=MESH,
        )
        copy.start()
        seconds.append(copy)
    if reps:
        part = lax.axis_index("rep")
        held[part] = pot * (1.0 / SCALE)
        for d, partner in enumerate(twins):
            copy = pltpu.make_async_remote_copy(
                src_ref=held.at[part], dst_ref=held.at[part],
                send_sem=rep_send.at[d], recv_sem=rep_recv.at[d],
                device_id=partner, device_id_type=MESH,
            )
            copy.start()
            seconds.append(copy)
    for copy in copies:
        copy.wait_send()
    for copy in seconds:
        copy.wait()
    out[...] = full[...]
    if reps:
        both[...] = held[...]


def column_potentials(n, reps, sums, call):
    last = call == ITERS - 1
    share, blk = sums.shape[0] // n, sums.shape[1]
    if n > DIRECT:
        pot = SHIFT - jnp.log2(lax.psum(sums, "roll") + FLOOR)
        if not last:
            return pot, None
        mine = lax.dynamic_slice_in_dim(pot, lax.axis_index("roll") * share, share, 0)
        return pot, lax.all_gather(mine, "rep") / SCALE
    sums = sums.reshape(n, share, blk)
    dma = pltpu.SemaphoreType.DMA
    vmem = pl.BlockSpec(memory_space=pltpu.VMEM)
    both = (reps, share, blk)
    outs = [jax.ShapeDtypeStruct(sums.shape, sums.dtype)]
    scratch = [pltpu.VMEM((n - 1, share, blk), jnp.float32), pltpu.VMEM((n, share, blk), jnp.float32)]
    if last:
        outs.append(jax.ShapeDtypeStruct(both, sums.dtype))
        scratch.append(pltpu.VMEM(both, jnp.float32))
    scratch += [dma((n - 1,))] * 4
    if last:
        scratch += [dma((reps - 1,))] * 2
    out = pl.pallas_call(
        functools.partial(column_kernel, n, reps if last else 0),
        out_shape=outs,
        in_specs=[vmem],
        out_specs=[vmem] * len(outs),
        scratch_shapes=scratch,
        compiler_params=pltpu.CompilerParams(
            collective_id=1 + call, has_side_effects=True, vmem_limit_bytes=MIB
        ),
        name="column_exchange_%d" % call,
    )(sums)
    return out[0].reshape(n * share, blk), out[1] if last else None


def row_kernel(reps, last, sums, *refs):
    outs, (landed, send_sem, recv_sem) = refs[:-3], refs[-3:]
    part = lax.axis_index("rep")
    partners = others("rep", reps)
    greet(partners)
    copies = []
    for d, partner in enumerate(partners):
        copy = pltpu.make_async_remote_copy(
            src_ref=sums, dst_ref=landed.at[d], send_sem=send_sem.at[d], recv_sem=recv_sem.at[d],
            device_id=partner, device_id_type=MESH,
        )
        copy.start()
        copies.append(copy)
    for copy in copies:
        copy.wait_recv()
    if last:
        heights, weighted = (
            sum((landed[d, k, part] for d in range(reps - 1)), sums[k, part]) for k in range(2)
        )
        heights = heights + FLOOR
        outs[0][...] = -(weighted + UNMATCHED * FLOOR) / heights
        outs[1][...] = (SHIFT - jnp.log2(heights)) * (1.0 / SCALE)
    else:
        total = sum((landed[d, 0] for d in range(reps - 1)), sums[0])
        outs[0][...] = SHIFT - jnp.log2(total + FLOOR)
    for copy in copies:
        copy.wait_send()


def row_totals(reps, sums, call):
    last = call == ITERS - 1
    sums = sums.reshape(sums.shape[0], reps, -1, sums.shape[2])
    dma = pltpu.SemaphoreType.DMA((reps - 1,))
    vmem = pl.BlockSpec(memory_space=pltpu.VMEM)
    shapes = [sums.shape[2:]] * 2 if last else [sums.shape[1:]]
    return pl.pallas_call(
        functools.partial(row_kernel, reps, last),
        out_shape=[jax.ShapeDtypeStruct(shape, sums.dtype) for shape in shapes],
        in_specs=[vmem],
        out_specs=[vmem] * len(shapes),
        scratch_shapes=[pltpu.VMEM((reps - 1,) + sums.shape, jnp.float32), dma, dma],
        compiler_params=pltpu.CompilerParams(
            collective_id=1 + ITERS + call, has_side_effects=True, vmem_limit_bytes=2 * MIB
        ),
        name="row_exchange_%d" % call,
    )(sums)


def body(rollout, demo, projection, location, pair_block, pair_count):
    blk = rollout.shape[0] // pair_block.shape[0]
    n = lax.axis_size("roll")
    reps = lax.axis_size("rep")
    if n <= DIRECT:
        v, vnorm, u, unorm, lists = gathered(
            n, reps, demo, rollout, projection, pair_block, pair_count, location
        )
    else:
        part = lax.axis_index("rep")
        demo_count = demo.shape[0] // blk
        share = demo_count // reps
        own_demo = lax.dynamic_slice_in_dim(demo, part * (share * blk), share * blk, 0)
        own_v = project(own_demo, projection)
        own_u = project(rollout, projection)
        v, vnorm = (lax.all_gather(a, "roll") for a in (own_v, norms(own_v, blk)))
        u, unorm = (lax.all_gather(a, "rep") for a in (own_u, norms(own_u, blk)))
        pairs, counts = (lax.all_gather(a, "rep", tiled=True) for a in (pair_block, pair_count))
        lists = listed(pairs, counts, location, demo_count, share, part)
    v, vnorm, u, unorm = (a.reshape(-1, a.shape[-1]) for a in (v, vnorm, u, unorm))

    stored = n <= DIRECT
    roll_pot = kept = None
    for iteration in range(ITERS):
        sums, *rest = run_pass("column", lists, u, v, unorm, vnorm, roll_pot, kept, stored)
        kept = rest[0] if rest else kept
        demo_pot, held_pot = column_potentials(n, reps, sums, iteration)
        kind = "final" if iteration == ITERS - 1 else "row"
        sums = run_pass(kind, lists, u, v, unorm, vnorm, demo_pot, kept, stored)[0]
        results = row_totals(reps, sums, iteration)
        roll_pot = results[0].reshape(unorm.shape) if kind == "row" else None
    return results[0].reshape(-1), results[1].reshape(-1), held_pot.reshape(-1)


def solution(mesh):
    placed = (
        P(("roll", "rep"), None),
        P("roll", None),
        P(),
        P(),
        P(("roll", "rep"), None),
        P(("roll", "rep")),
    )
    return jax.shard_map(
        body,
        mesh=mesh,
        in_specs=placed,
        out_specs=(P(("roll", "rep")), P(("roll", "rep")), P("roll")),
        check_vma=False,
    )
```

```python
import functools
import math

import jax
import jax.numpy as jnp
from jax import lax
from jax.experimental import pallas as pl
from jax.experimental.pallas import tpu as pltpu
from jax.sharding import PartitionSpec as P

ITERS = 2
EPSILON = 0.02
UNMATCHED = 2.0
SLACK = -100.0
LOG2E = math.log2(math.e)
SCALE = LOG2E / EPSILON
SHIFT = 50.0 * LOG2E
FLOOR = math.exp(SLACK + 50.0)
UNROLL = 4
DIRECT = 16
CHUNKS = 4
MIB = 1024 * 1024
MESH = pl.DeviceIdType.MESH


def pass_kernel(kind, fresh, stored, lists_ref, *refs):
    refs = list(refs)
    reads = stored and not fresh
    if reads:
        kept = refs.pop(0)
    else:
        u_ref, v_ref, unorm_ref, vnorm_ref = refs[:4]
        refs = refs[4:]
    pot_ref = None if fresh else refs.pop(0)
    out_ref = refs.pop(0)
    if stored and fresh:
        kept = refs.pop(0)
    sums_ref = refs.pop()
    if kind == "final":
        wsums_ref = refs.pop()
        wsums_ref[...] = jnp.zeros_like(wsums_ref)
    sums_ref[...] = jnp.zeros_like(sums_ref)
    blk = out_ref.shape[-1]
    by_column = kind == "column"
    roll_blocks = (refs[0] if refs else sums_ref).shape[0] // blk

    if not reads:
        row_norm = refs.pop(0)
        feats = u_ref.shape[1]
        unit = SCALE / feats
        roll_blocks = unorm_ref.shape[0]

    def spread(source, factor, target):
        def one(b, carry):
            line = source[pl.ds(b, 1), :] * factor
            rows = pl.ds(pl.multiple_of(b * blk, blk), blk)
            target[rows, :] = jnp.transpose(jnp.broadcast_to(line, (blk, blk)))
            return carry

        lax.fori_loop(0, roll_blocks, one, 0, unroll=8)

    if not reads:
        spread(unorm_ref, -unit, row_norm)
    if by_column and not fresh:
        row_pot = refs.pop(0)
        spread(pot_ref, 1.0, row_pot)

    total = lists_ref[2, 0]

    def step(k, carry):
        parts = []
        for p in range(UNROLL):
            at = k * UNROLL + p
            b = lists_ref[0, at]
            t = lists_ref[1, at]
            live = jnp.where(at < total, SHIFT, -1e30)
            rows = pl.ds(pl.multiple_of(b * blk, blk), blk)
            here = pl.ds(pl.multiple_of(at * blk, blk), blk)
            if reads:
                y = kept[here, :]
            else:
                crossed = lax.dot_general(
                    u_ref[rows, :],
                    v_ref[pl.ds(pl.multiple_of(t * feats, feats), feats), :],
                    (((1,), (0,)), ((), ())),
                    preferred_element_type=jnp.float32,
                )
                y = crossed * (2.0 * unit) + row_norm[rows, :] + vnorm_ref[pl.ds(t, 1), :] * (-unit)
                if stored:
                    kept[here, :] = y
            if by_column:
                x = y + live if fresh else y + row_pot[rows, :] + live
                parts.append((t, jnp.sum(jnp.exp2(x).reshape(blk // 8, 8, blk), axis=0)))
            else:
                e = jnp.exp2(y + (pot_ref[pl.ds(t, 1), :] + live))
                parts.append((rows, e, e * y if kind == "final" else None))
        for where, e, *weighted in parts:
            if by_column:
                at8 = pl.ds(pl.multiple_of(where * 8, 8), 8)
                sums_ref[at8, :] = sums_ref[at8, :] + e
            else:
                sums_ref[where, :] = sums_ref[where, :] + e
                if kind == "final":
                    wsums_ref[where, :] = wsums_ref[where, :] + weighted[0]
        return carry

    lax.fori_loop(0, (total + UNROLL - 1) // UNROLL, step, 0)

    if by_column:
        out_ref[...] = jnp.sum(sums_ref[...].reshape(out_ref.shape[0], 8, blk), axis=1)
    else:

        def finish(b, carry):
            rows = pl.ds(pl.multiple_of(b * blk, blk), blk)
            out_ref[0, pl.ds(b, 1), :] = jnp.sum(jnp.transpose(sums_ref[rows, :]), axis=0, keepdims=True)
            if kind == "final":
                out_ref[1, pl.ds(b, 1), :] = jnp.sum(
                    jnp.transpose(wsums_ref[rows, :]), axis=0, keepdims=True
                ) * (-1.0 / SCALE)
            return carry

        lax.fori_loop(0, roll_blocks, finish, 0, unroll=8)


def run_pass(kind, lists, u, v, unorm, vnorm, pot, kept, stored):
    fresh = pot is None
    roll_blocks, blk = unorm.shape
    targets = vnorm.shape[0]
    pairs = lists.shape[1] - 128
    smem = pl.BlockSpec(memory_space=pltpu.SMEM)
    vmem = pl.BlockSpec(memory_space=pltpu.VMEM)
    frames = pltpu.VMEM((roll_blocks * blk, blk), jnp.float32)
    by_column = kind == "column"
    reads = stored and not fresh
    args = [kept] if reads else [u, v, unorm, vnorm]
    if not fresh:
        args.append(pot)
    if by_column:
        outs = [jax.ShapeDtypeStruct((targets, blk), jnp.float32)]
        sums = [pltpu.VMEM((targets * 8, blk), jnp.float32)]
    else:
        outs = [jax.ShapeDtypeStruct((2 if kind == "final" else 1, roll_blocks, blk), jnp.float32)]
        sums = [frames] * (2 if kind == "final" else 1)
    if stored and fresh:
        outs.append(jax.ShapeDtypeStruct(((pairs + UNROLL) * blk, blk), jnp.float32))
    scratch = ([] if reads else [frames]) + ([frames] if by_column and not fresh else []) + sums
    held = sum(math.prod(a.shape) * a.dtype.itemsize for a in scratch + ([] if stored else args + outs))
    return pl.pallas_call(
        functools.partial(pass_kernel, kind, fresh, stored),
        out_shape=outs,
        in_specs=[smem] + [vmem] * len(args),
        out_specs=[vmem] * len(outs),
        scratch_shapes=scratch,
        compiler_params=pltpu.CompilerParams(vmem_limit_bytes=held + 2 * MIB),
        cost_estimate=pl.CostEstimate(
            flops=0 if reads else pairs * blk * blk * u.shape[1],
            bytes_accessed=2 * v.size,
            transcendentals=pairs * blk * blk // 2,
        ),
        name="pass_" + kind,
    )(lists, *args)


def listed(pair_block, pair_count, location, demo_count, share, part):
    roll_blocks, slots = pair_block.shape
    n = roll_blocks * slots
    names = jnp.arange(location.shape[0], dtype=jnp.int32)
    flat = pair_block.reshape(n)
    stored = jnp.sum(jnp.where(flat[:, None] == names[None, :], location[None, :], 0), axis=1)
    active = (jnp.arange(slots, dtype=jnp.int32)[None, :] < pair_count[:, None]).reshape(n)
    local = stored % demo_count
    mine = active & (local // share == part)
    target = (stored // demo_count) * share + local % share
    ids = jnp.arange(n, dtype=jnp.int32)
    rank = jnp.sum((mine[None, :] & (ids[None, :] < ids[:, None])).astype(jnp.int32), axis=1)
    place = jnp.where(mine, rank, -1)
    hit = place[None, :] == ids[:, None]
    home = jnp.sum(jnp.where(hit, (ids // slots)[None, :], 0), axis=1)
    target = jnp.sum(jnp.where(hit, target[None, :], 0), axis=1)
    total = jnp.sum(mine.astype(jnp.int32)).reshape(1)
    lists = jnp.stack([home, target, jnp.broadcast_to(total, (n,))])
    return jnp.pad(lists, ((0, 0), (0, 128)))


def project(frames, projection):
    return jnp.dot(frames, projection, preferred_element_type=jnp.float32).astype(jnp.bfloat16)


def norms(codes, blk):
    wide = codes.astype(jnp.float32)
    return jnp.sum(wide * wide, axis=1).reshape(-1, blk)


def greet(partners):
    barrier = pltpu.get_barrier_semaphore()
    for partner in partners:
        pl.semaphore_signal(barrier, inc=1, device_id=partner, device_id_type=MESH)
    pl.semaphore_wait(barrier, len(partners))


def others(axis, size):
    me = lax.axis_index(axis)
    return [{axis: lax.rem(me + d, size)} for d in range(1, size)]


def block_norms(codes):
    wide = codes.astype(jnp.float32)
    square = wide * wide
    high = square.astype(jnp.bfloat16)
    low = (square - high.astype(jnp.float32)).astype(jnp.bfloat16)
    ones = jnp.ones((8, codes.shape[1]), jnp.bfloat16)
    dims = (((1,), (1,)), ((), ()))
    total = lax.dot_general(ones, high, dims, preferred_element_type=jnp.float32)
    total = total + lax.dot_general(ones, low, dims, preferred_element_type=jnp.float32)
    return total[0:1, :]


def packed_pairs(pairs, location, slots, demo_count, share, part, width):
    blocks = pairs.shape[0]
    names = lax.broadcasted_iota(jnp.int32, (blocks, 128), 1).astype(jnp.float32)
    places = lax.broadcasted_iota(jnp.int32, (blocks, width), 1).astype(jnp.float32)
    number = lax.broadcasted_iota(jnp.int32, (blocks, width), 0).astype(jnp.float32)
    count = pairs[:, slots : slots + 1]
    where_held = location.astype(jnp.float32)
    mine, target = [], []
    for s in range(slots):
        found = jnp.zeros((blocks, 128), jnp.float32)
        for k in range(location.shape[0]):
            hit = pairs[:, s : s + 1] - 128.0 * k == names
            found = found + jnp.where(hit, where_held[k : k + 1, :], 0.0)
        stored = jnp.sum(found, axis=1, keepdims=True)
        owner = jnp.floor((stored + 0.5) * (1.0 / demo_count))
        local = stored - owner * demo_count
        side = jnp.floor((local + 0.5) * (1.0 / share))
        mine.append(jnp.where((count > s) & (side == part.astype(jnp.float32)), 1.0, 0.0))
        target.append(owner * share + local - side * share)
    in_row = sum(mine)
    below = lax.broadcasted_iota(jnp.int32, (blocks, blocks), 1) < lax.broadcasted_iota(jnp.int32, (blocks, blocks), 0)
    spread = jnp.broadcast_to(in_row, (blocks, 128)).astype(jnp.bfloat16)
    before = jnp.dot(below.astype(jnp.float32).astype(jnp.bfloat16), spread, preferred_element_type=jnp.float32)
    rank = before[:, 0:1]
    homes = jnp.zeros((blocks, width), jnp.float32)
    targets = jnp.zeros((blocks, width), jnp.float32)
    for s in range(slots):
        hit = (rank == places) & (mine[s] > 0.5)
        homes = homes + jnp.where(hit, number, 0.0)
        targets = targets + jnp.where(hit, target[s], 0.0)
        rank = rank + mine[s]
    total = jnp.sum(jnp.broadcast_to(in_row, (blocks, width)), axis=0, keepdims=True)
    rows = [jnp.sum(homes, axis=0, keepdims=True), jnp.sum(targets, axis=0, keepdims=True), total]
    return [row.astype(jnp.int32) for row in rows]


def gather_kernel(n, reps, slots, *refs):
    demo, rollout, projection_hbm, pair_block, pair_count, location_hbm = refs[:6]
    v, vnorm, u, unorm, lists = refs[6:11]
    (demo_in, rollout_in, projection, location, block_in, count_in, own_pairs, own_v, own_vnorm, own_u, own_unorm, pairs,
     ring_send, ring_recv, side_send, side_recv, norm_send, norm_recv, rep_send, rep_recv, home) = refs[11:]
    me = lax.axis_index("roll")
    part = lax.axis_index("rep")
    chips = n // 2
    hops = chips // 2
    core = lax.rem(me, 2)
    chip = me // 2
    odd = lax.rem(chip, 2)
    place = (1 - odd) * (chip // 2) + odd * (chips - 1 - chip // 2)

    def at_place(p):
        p = lax.rem(p + 2 * chips, chips)
        high = p // hops
        return ((1 - high) * (2 * p) + high * (2 * (chips - 1 - p) + 1)) * 2 + core

    twin = {"roll": me + 1 - 2 * core}
    ways = ({"roll": at_place(place + 1)}, {"roll": at_place(place - 1)})
    rows = own_v.shape[0] // CHUNKS
    feats = projection.shape[1]
    share, blk = own_vnorm.shape
    own_blocks = own_unorm.shape[0]
    near = others("roll", n) + others("rep", reps)
    fetch_demo = pltpu.make_async_copy(demo.at[pl.ds(part * (share * blk), share * blk)], demo_in, home.at[4])
    fetch_demo.start()
    fetches = [
        pltpu.make_async_copy(source, target, home.at[6 + k])
        for k, (source, target) in enumerate((
            (projection_hbm, projection),
            (pair_block, block_in),
            (pair_count, count_in),
            (location_hbm, location),
        ))
    ]
    for fetch in fetches:
        fetch.start()
    fetch_rollout = pltpu.make_async_copy(rollout, rollout_in, home.at[5])
    fetch_rollout.start()
    barrier = pltpu.get_barrier_semaphore()
    for partner in near:
        pl.semaphore_signal(barrier, inc=1, device_id=partner, device_id_type=MESH)
    fetch_demo.wait()
    for fetch in fetches:
        fetch.wait()
    own_pairs[...] = jnp.zeros_like(own_pairs)
    own_pairs[0:slots, 0 : block_in.shape[1]] = block_in[...]
    own_pairs[slots : slots + 1, 0 : count_in.shape[1]] = count_in[...]
    turned = jnp.transpose(projection[...])
    for b in range(share):
        own_v[b * feats : (b + 1) * feats, :] = lax.dot_general(
            turned, demo_in[b * blk : (b + 1) * blk, :], (((1,), (1,)), ((), ())),
            preferred_element_type=jnp.float32,
        ).astype(jnp.bfloat16)
    pl.semaphore_wait(barrier, len(near))

    waits = []

    def origin(way, s):
        return at_place(place - s) if way == 0 else at_place(place + s)

    def chunk(s, way, half):
        piece = pl.ds(half * rows, rows)
        if s == 0:
            return own_v.at[piece], v.at[me, piece]
        block = origin(way, s)
        return v.at[block, piece], v.at[block, piece]

    def send(s, way, half):
        source, target = chunk(s, way, half)
        copy = pltpu.make_async_remote_copy(
            src_ref=source, dst_ref=target,
            send_sem=ring_send.at[way, s, half], recv_sem=ring_recv.at[way, s, half],
            device_id=ways[way], device_id_type=MESH,
        )
        copy.start()
        return copy

    def cross(s, way, half):
        source, target = chunk(s, way, half)
        copy = pltpu.make_async_remote_copy(
            src_ref=source, dst_ref=target,
            send_sem=side_send.at[way, s, half], recv_sem=side_recv.at[way, s, half],
            device_id=twin, device_id_type=MESH,
        )
        copy.start()
        waits.append(copy)

    def travels(s, way, half):
        return s < hops - 1 or (s == hops - 1 and half * 2 // CHUNKS == way)

    moving = {}
    for half in range(CHUNKS):
        for way in range(2):
            if travels(0, way, half):
                moving[0, way, half] = send(0, way, half)

    def spread(source, target, axis, which, sends, recvs):
        started = []
        for d, partner in enumerate(others(axis, reps if axis == "rep" else n)):
            copy = pltpu.make_async_remote_copy(
                src_ref=source, dst_ref=target,
                send_sem=sends.at[which, d], recv_sem=recvs.at[which, d],
                device_id=partner, device_id_type=MESH,
            )
            copy.start()
            started.append(copy)
        return started

    pair_copies = spread(own_pairs, pairs.at[part], "rep", 0, rep_send, rep_recv)
    pairs[part] = own_pairs[...]
    for half in range(CHUNKS):
        cross(0, 0, half)
    fetch_rollout.wait()

    def do_rollout(b, carry):
        rows_b = pl.ds(pl.multiple_of(b * blk, blk), blk)
        codes = jnp.dot(
            rollout_in[rows_b, :], projection[...], preferred_element_type=jnp.float32
        ).astype(jnp.bfloat16)
        own_u[rows_b, :] = codes
        own_unorm[pl.ds(b, 1), :] = block_norms(codes)
        return carry

    lax.fori_loop(0, own_blocks, do_rollout, 0)

    def send_rollout(q):
        piece = pl.ds(q * (own_u.shape[0] // hops), own_u.shape[0] // hops)
        return spread(own_u.at[piece], u.at[part, piece], "rep", 2 + q, rep_send, rep_recv)

    waits += send_rollout(0)
    waits += spread(own_unorm, unorm.at[part], "rep", 1, rep_send, rep_recv)

    def do_demo(b, carry):
        wide = own_v[pl.ds(pl.multiple_of(b * feats, feats), feats), :].astype(jnp.float32)
        own_vnorm[pl.ds(b, 1), :] = jnp.sum(wide * wide, axis=0, keepdims=True)
        return carry

    lax.fori_loop(0, share, do_demo, 0)
    waits += spread(own_vnorm, vnorm.at[me], "roll", 0, norm_send, norm_recv)
    stays = []
    for k, (source, target) in enumerate(
        ((own_v, v.at[me]), (own_vnorm, vnorm.at[me]), (own_u, u.at[part]), (own_unorm, unorm.at[part]))
    ):
        copy = pltpu.make_async_copy(source, target, home.at[k])
        copy.start()
        stays.append(copy)
    for copy in pair_copies:
        copy.wait()
    square = [
        jnp.concatenate([pairs[r].astype(jnp.float32), jnp.zeros((128 - pairs.shape[1], 128), jnp.float32)], axis=0)
        for r in range(reps)
    ]
    everyone = jnp.concatenate([jnp.transpose(a)[0:own_blocks, :] for a in square], axis=0)
    found = packed_pairs(everyone, location[...], slots, share * reps, share, part, lists.shape[1])
    lists[...] = jnp.zeros_like(lists)
    for k, row in enumerate(found):
        lists[k : k + 1, :] = row
    for s in range(1, hops + 1):
        for half in range(CHUNKS):
            for way in range(2):
                if (s - 1, way, half) not in moving:
                    continue
                moving[s - 1, way, half].wait_recv()
                if travels(s, way, half):
                    moving[s, way, half] = send(s, way, half)
                cross(s, way, half)
        if s < hops:
            waits += send_rollout(s)
    for copy in moving.values():
        copy.wait_send()
    for copy in stays:
        copy.wait()
    for copy in waits:
        copy.wait()


def gathered(n, reps, demo, rollout, projection, pair_block, pair_count, location):
    hops = n // 4
    own_blocks, slots = pair_block.shape
    blk = rollout.shape[0] // own_blocks
    feats = projection.shape[1]
    share = demo.shape[0] // blk // reps
    location = location.reshape(-1, 128)
    own_pairs = (slots // 8 * 8 + 8, 128)
    hbm = pl.BlockSpec(memory_space=pltpu.HBM)
    anywhere = pl.BlockSpec(memory_space=pl.ANY)
    vmem = pl.BlockSpec(memory_space=pltpu.VMEM)
    dma = pltpu.SemaphoreType.DMA
    wide, code = jnp.float32, jnp.bfloat16
    return pl.pallas_call(
        functools.partial(gather_kernel, n, reps, slots),
        out_shape=[
            jax.ShapeDtypeStruct((n, share * feats, blk), code),
            jax.ShapeDtypeStruct((n, share, blk), wide),
            jax.ShapeDtypeStruct((reps, own_blocks * blk, feats), code),
            jax.ShapeDtypeStruct((reps, own_blocks, blk), wide),
            jax.ShapeDtypeStruct((8, reps * own_blocks * slots + 128), jnp.int32),
        ],
        in_specs=[hbm] * 6,
        out_specs=[anywhere] * 4 + [vmem],
        scratch_shapes=[
            pltpu.VMEM((share * blk, feats), code),
            pltpu.VMEM(rollout.shape, code),
            pltpu.VMEM(projection.shape, code),
            pltpu.VMEM(location.shape, jnp.int32),
            pltpu.VMEM((slots, own_blocks), jnp.int32),
            pltpu.VMEM((1, own_blocks), jnp.int32),
            pltpu.VMEM(own_pairs, jnp.int32),
            pltpu.VMEM((share * feats, blk), code),
            pltpu.VMEM((share, blk), wide),
            pltpu.VMEM((own_blocks * blk, feats), code),
            pltpu.VMEM((own_blocks, blk), wide),
            pltpu.VMEM((reps,) + own_pairs, jnp.int32),
            dma((2, hops, CHUNKS)), dma((2, hops, CHUNKS)),
            dma((2, hops + 1, CHUNKS)), dma((2, hops + 1, CHUNKS)),
            dma((1, n - 1)), dma((1, n - 1)),
            dma((2 + hops, reps - 1)), dma((2 + hops, reps - 1)),
            dma((10,)),
        ],
        compiler_params=pltpu.CompilerParams(
            collective_id=0, has_side_effects=True, vmem_limit_bytes=8 * MIB
        ),
        name="gather_codes",
    )(*(
        pltpu.with_memory_space_constraint(a, pltpu.HBM)
        for a in (demo, rollout, projection, pair_block.T, pair_count[None, :], location)
    ))


def column_kernel(n, reps, sums, *refs):
    if reps:
        out, both, landed, full, held, first_send, first_recv, second_send, second_recv, rep_send, rep_recv = refs
    else:
        out, landed, full, first_send, first_recv, second_send, second_recv = refs
    me = lax.axis_index("roll")
    partners = others("roll", n)
    twins = others("rep", reps) if reps else []
    greet(partners + twins)
    copies = []
    for d, partner in enumerate(partners):
        copy = pltpu.make_async_remote_copy(
            src_ref=sums.at[partner["roll"]], dst_ref=landed.at[d],
            send_sem=first_send.at[d], recv_sem=first_recv.at[d],
            device_id=partner, device_id_type=MESH,
        )
        copy.start()
        copies.append(copy)
    total = sums[me]
    for d, copy in enumerate(copies):
        copy.wait_recv()
        total = total + landed[d]
    pot = SHIFT - jnp.log2(total + FLOOR)
    full[me] = pot
    seconds = []
    for d, partner in enumerate(partners):
        copy = pltpu.make_async_remote_copy(
            src_ref=full.at[me], dst_ref=full.at[me],
            send_sem=second_send.at[d], recv_sem=second_recv.at[d],
            device_id=partner, device_id_type=MESH,
        )
        copy.start()
        seconds.append(copy)
    if reps:
        part = lax.axis_index("rep")
        held[part] = pot * (1.0 / SCALE)
        for d, partner in enumerate(twins):
            copy = pltpu.make_async_remote_copy(
                src_ref=held.at[part], dst_ref=held.at[part],
                send_sem=rep_send.at[d], recv_sem=rep_recv.at[d],
                device_id=partner, device_id_type=MESH,
            )
            copy.start()
            seconds.append(copy)
    for copy in copies:
        copy.wait_send()
    for copy in seconds:
        copy.wait()
    out[...] = full[...]
    if reps:
        both[...] = held[...]


def column_potentials(n, reps, sums, call):
    last = call == ITERS - 1
    share, blk = sums.shape[0] // n, sums.shape[1]
    if n > DIRECT:
        pot = SHIFT - jnp.log2(lax.psum(sums, "roll") + FLOOR)
        if not last:
            return pot, None
        mine = lax.dynamic_slice_in_dim(pot, lax.axis_index("roll") * share, share, 0)
        return pot, lax.all_gather(mine, "rep") / SCALE
    sums = sums.reshape(n, share, blk)
    dma = pltpu.SemaphoreType.DMA
    vmem = pl.BlockSpec(memory_space=pltpu.VMEM)
    both = (reps, share, blk)
    outs = [jax.ShapeDtypeStruct(sums.shape, sums.dtype)]
    scratch = [pltpu.VMEM((n - 1, share, blk), jnp.float32), pltpu.VMEM((n, share, blk), jnp.float32)]
    if last:
        outs.append(jax.ShapeDtypeStruct(both, sums.dtype))
        scratch.append(pltpu.VMEM(both, jnp.float32))
    scratch += [dma((n - 1,))] * 4
    if last:
        scratch += [dma((reps - 1,))] * 2
    out = pl.pallas_call(
        functools.partial(column_kernel, n, reps if last else 0),
        out_shape=outs,
        in_specs=[vmem],
        out_specs=[vmem] * len(outs),
        scratch_shapes=scratch,
        compiler_params=pltpu.CompilerParams(
            collective_id=1 + call, has_side_effects=True, vmem_limit_bytes=MIB
        ),
        name="column_exchange_%d" % call,
    )(sums)
    return out[0].reshape(n * share, blk), out[1] if last else None


def row_kernel(reps, last, sums, *refs):
    outs, (landed, send_sem, recv_sem) = refs[:-3], refs[-3:]
    part = lax.axis_index("rep")
    partners = others("rep", reps)
    greet(partners)
    copies = []
    for d, partner in enumerate(partners):
        copy = pltpu.make_async_remote_copy(
            src_ref=sums, dst_ref=landed.at[d], send_sem=send_sem.at[d], recv_sem=recv_sem.at[d],
            device_id=partner, device_id_type=MESH,
        )
        copy.start()
        copies.append(copy)
    for copy in copies:
        copy.wait_recv()
    if last:
        heights, weighted = (
            sum((landed[d, k, part] for d in range(reps - 1)), sums[k, part]) for k in range(2)
        )
        heights = heights + FLOOR
        outs[0][...] = -(weighted + UNMATCHED * FLOOR) / heights
        outs[1][...] = (SHIFT - jnp.log2(heights)) * (1.0 / SCALE)
    else:
        total = sum((landed[d, 0] for d in range(reps - 1)), sums[0])
        outs[0][...] = SHIFT - jnp.log2(total + FLOOR)
    for copy in copies:
        copy.wait_send()


def row_totals(reps, sums, call):
    last = call == ITERS - 1
    sums = sums.reshape(sums.shape[0], reps, -1, sums.shape[2])
    dma = pltpu.SemaphoreType.DMA((reps - 1,))
    vmem = pl.BlockSpec(memory_space=pltpu.VMEM)
    shapes = [sums.shape[2:]] * 2 if last else [sums.shape[1:]]
    return pl.pallas_call(
        functools.partial(row_kernel, reps, last),
        out_shape=[jax.ShapeDtypeStruct(shape, sums.dtype) for shape in shapes],
        in_specs=[vmem],
        out_specs=[vmem] * len(shapes),
        scratch_shapes=[pltpu.VMEM((reps - 1,) + sums.shape, jnp.float32), dma, dma],
        compiler_params=pltpu.CompilerParams(
            collective_id=1 + ITERS + call, has_side_effects=True, vmem_limit_bytes=2 * MIB
        ),
        name="row_exchange_%d" % call,
    )(sums)


def body(rollout, demo, projection, location, pair_block, pair_count):
    blk = rollout.shape[0] // pair_block.shape[0]
    n = lax.axis_size("roll")
    reps = lax.axis_size("rep")
    if n <= DIRECT:
        v, vnorm, u, unorm, lists = gathered(
            n, reps, demo, rollout, projection, pair_block, pair_count, location
        )
    else:
        part = lax.axis_index("rep")
        demo_count = demo.shape[0] // blk
        share = demo_count // reps
        own_demo = lax.dynamic_slice_in_dim(demo, part * (share * blk), share * blk, 0)
        own_v = project(own_demo, projection)
        own_u = project(rollout, projection)
        flipped = own_v.reshape(share, blk, -1).transpose(0, 2, 1).reshape(-1, blk)
        v, vnorm = (lax.all_gather(a, "roll") for a in (flipped, norms(own_v, blk)))
        u, unorm = (lax.all_gather(a, "rep") for a in (own_u, norms(own_u, blk)))
        pairs, counts = (lax.all_gather(a, "rep", tiled=True) for a in (pair_block, pair_count))
        lists = listed(pairs, counts, location, demo_count, share, part)
    v, vnorm, u, unorm = (a.reshape(-1, a.shape[-1]) for a in (v, vnorm, u, unorm))

    stored = n <= DIRECT
    roll_pot = kept = None
    for iteration in range(ITERS):
        sums, *rest = run_pass("column", lists, u, v, unorm, vnorm, roll_pot, kept, stored)
        kept = rest[0] if rest else kept
        demo_pot, held_pot = column_potentials(n, reps, sums, iteration)
        kind = "final" if iteration == ITERS - 1 else "row"
        sums = run_pass(kind, lists, u, v, unorm, vnorm, demo_pot, kept, stored)[0]
        results = row_totals(reps, sums, iteration)
        roll_pot = results[0].reshape(unorm.shape) if kind == "row" else None
    return results[0].reshape(-1), results[1].reshape(-1), held_pot.reshape(-1)


def solution(mesh):
    placed = (
        P(("roll", "rep"), None),
        P("roll", None),
        P(),
        P(),
        P(("roll", "rep"), None),
        P(("roll", "rep")),
    )
    return jax.shard_map(
        body,
        mesh=mesh,
        in_specs=placed,
        out_specs=(P(("roll", "rep")), P(("roll", "rep")), P("roll")),
        check_vma=False,
    )
```

```python
import functools
import math

import jax
import jax.numpy as jnp
from jax import lax
from jax.experimental import pallas as pl
from jax.experimental.pallas import tpu as pltpu
from jax.sharding import PartitionSpec as P

ITERS = 2
EPSILON = 0.02
UNMATCHED = 2.0
SLACK = -100.0
LOG2E = math.log2(math.e)
SCALE = LOG2E / EPSILON
SHIFT = 50.0 * LOG2E
FLOOR = math.exp(SLACK + 50.0)
UNROLL = 4
DIRECT = 16
CHUNKS = 4
MIB = 1024 * 1024
MESH = pl.DeviceIdType.MESH


def pass_kernel(kind, fresh, stored, lists_ref, *refs):
    refs = list(refs)
    if stored:
        kept = refs.pop(0)
    else:
        u_ref, v_ref, unorm_ref, vnorm_ref = refs[:4]
        refs = refs[4:]
    pot_ref = None if fresh else refs.pop(0)
    out_ref = refs.pop(0)
    sums_ref = refs.pop()
    if kind == "final":
        wsums_ref = refs.pop()
        wsums_ref[...] = jnp.zeros_like(wsums_ref)
    sums_ref[...] = jnp.zeros_like(sums_ref)
    blk = out_ref.shape[-1]
    by_column = kind == "column"
    roll_blocks = (refs[0] if refs else sums_ref).shape[0] // blk

    if not stored:
        row_norm = refs.pop(0)
        feats = u_ref.shape[1]
        unit = SCALE / feats
        roll_blocks = unorm_ref.shape[0]

    def spread(source, factor, target):
        def one(b, carry):
            line = source[pl.ds(b, 1), :] * factor
            rows = pl.ds(pl.multiple_of(b * blk, blk), blk)
            target[rows, :] = jnp.transpose(jnp.broadcast_to(line, (blk, blk)))
            return carry

        lax.fori_loop(0, roll_blocks, one, 0, unroll=8)

    if not stored:
        spread(unorm_ref, -unit, row_norm)
    if by_column and not fresh:
        row_pot = refs.pop(0)
        spread(pot_ref, 1.0, row_pot)

    total = lists_ref[2, 0]

    def step(k, carry):
        parts = []
        for p in range(UNROLL):
            at = k * UNROLL + p
            b = lists_ref[0, at]
            t = lists_ref[1, at]
            live = jnp.where(at < total, SHIFT, -1e30)
            rows = pl.ds(pl.multiple_of(b * blk, blk), blk)
            if stored:
                y = kept[pl.ds(pl.multiple_of(lists_ref[3, at] * blk, blk), blk), :]
            else:
                crossed = lax.dot_general(
                    u_ref[rows, :],
                    v_ref[pl.ds(pl.multiple_of(t * feats, feats), feats), :],
                    (((1,), (0,)), ((), ())),
                    preferred_element_type=jnp.float32,
                )
                y = crossed * (2.0 * unit) + row_norm[rows, :] + vnorm_ref[pl.ds(t, 1), :] * (-unit)
            if by_column:
                x = y + live if fresh else y + row_pot[rows, :] + live
                parts.append((t, jnp.sum(jnp.exp2(x).reshape(blk // 8, 8, blk), axis=0)))
            else:
                e = jnp.exp2(y + (pot_ref[pl.ds(t, 1), :] + live))
                parts.append((rows, e, e * y if kind == "final" else None))
        for where, e, *weighted in parts:
            if by_column:
                at8 = pl.ds(pl.multiple_of(where * 8, 8), 8)
                sums_ref[at8, :] = sums_ref[at8, :] + e
            else:
                sums_ref[where, :] = sums_ref[where, :] + e
                if kind == "final":
                    wsums_ref[where, :] = wsums_ref[where, :] + weighted[0]
        return carry

    lax.fori_loop(0, (total + UNROLL - 1) // UNROLL, step, 0)

    if by_column:
        out_ref[...] = jnp.sum(sums_ref[...].reshape(out_ref.shape[0], 8, blk), axis=1)
    else:

        def finish(b, carry):
            rows = pl.ds(pl.multiple_of(b * blk, blk), blk)
            out_ref[0, pl.ds(b, 1), :] = jnp.sum(jnp.transpose(sums_ref[rows, :]), axis=0, keepdims=True)
            if kind == "final":
                out_ref[1, pl.ds(b, 1), :] = jnp.sum(
                    jnp.transpose(wsums_ref[rows, :]), axis=0, keepdims=True
                ) * (-1.0 / SCALE)
            return carry

        lax.fori_loop(0, roll_blocks, finish, 0, unroll=8)


def run_pass(kind, sizes, lists, data, pot, stored):
    fresh = pot is None
    roll_blocks, targets, blk = sizes
    pairs = lists.shape[1] - 128
    smem = pl.BlockSpec(memory_space=pltpu.SMEM)
    vmem = pl.BlockSpec(memory_space=pltpu.VMEM)
    frames = pltpu.VMEM((roll_blocks * blk, blk), jnp.float32)
    by_column = kind == "column"
    args = list(data)
    if not fresh:
        args.append(pot)
    if by_column:
        outs = [jax.ShapeDtypeStruct((targets, blk), jnp.float32)]
        sums = [pltpu.VMEM((targets * 8, blk), jnp.float32)]
    else:
        outs = [jax.ShapeDtypeStruct((2 if kind == "final" else 1, roll_blocks, blk), jnp.float32)]
        sums = [frames] * (2 if kind == "final" else 1)
    scratch = ([] if stored else [frames]) + ([frames] if by_column and not fresh else []) + sums
    held = sum(math.prod(a.shape) * a.dtype.itemsize for a in scratch + ([] if stored else args + outs))
    return pl.pallas_call(
        functools.partial(pass_kernel, kind, fresh, stored),
        out_shape=outs,
        in_specs=[smem] + [vmem] * len(args),
        out_specs=[vmem] * len(outs),
        scratch_shapes=scratch,
        compiler_params=pltpu.CompilerParams(vmem_limit_bytes=held + 2 * MIB),
        cost_estimate=pl.CostEstimate(
            flops=pairs * blk * blk * (4 if stored else data[0].shape[1]),
            bytes_accessed=pairs * blk * blk * 4,
            transcendentals=pairs * blk * blk // 2,
        ),
        name="pass_" + kind,
    )(lists, *args)


def listed(pair_block, pair_count, location, demo_count, share, part):
    roll_blocks, slots = pair_block.shape
    n = roll_blocks * slots
    names = jnp.arange(location.shape[0], dtype=jnp.int32)
    flat = pair_block.reshape(n)
    stored = jnp.sum(jnp.where(flat[:, None] == names[None, :], location[None, :], 0), axis=1)
    active = (jnp.arange(slots, dtype=jnp.int32)[None, :] < pair_count[:, None]).reshape(n)
    local = stored % demo_count
    mine = active & (local // share == part)
    target = (stored // demo_count) * share + local % share
    ids = jnp.arange(n, dtype=jnp.int32)
    rank = jnp.sum((mine[None, :] & (ids[None, :] < ids[:, None])).astype(jnp.int32), axis=1)
    place = jnp.where(mine, rank, -1)
    hit = place[None, :] == ids[:, None]
    home = jnp.sum(jnp.where(hit, (ids // slots)[None, :], 0), axis=1)
    target = jnp.sum(jnp.where(hit, target[None, :], 0), axis=1)
    total = jnp.sum(mine.astype(jnp.int32)).reshape(1)
    lists = jnp.stack([home, target, jnp.broadcast_to(total, (n,))])
    return jnp.pad(lists, ((0, 0), (0, 128)))


def project(frames, projection):
    return jnp.dot(frames, projection, preferred_element_type=jnp.float32).astype(jnp.bfloat16)


def norms(codes, blk):
    wide = codes.astype(jnp.float32)
    return jnp.sum(wide * wide, axis=1).reshape(-1, blk)


def greet(partners):
    barrier = pltpu.get_barrier_semaphore()
    for partner in partners:
        pl.semaphore_signal(barrier, inc=1, device_id=partner, device_id_type=MESH)
    pl.semaphore_wait(barrier, len(partners))


def others(axis, size):
    me = lax.axis_index(axis)
    return [{axis: lax.rem(me + d, size)} for d in range(1, size)]


def block_norms(codes):
    wide = codes.astype(jnp.float32)
    square = wide * wide
    high = square.astype(jnp.bfloat16)
    low = (square - high.astype(jnp.float32)).astype(jnp.bfloat16)
    ones = jnp.ones((8, codes.shape[1]), jnp.bfloat16)
    dims = (((1,), (1,)), ((), ()))
    total = lax.dot_general(ones, high, dims, preferred_element_type=jnp.float32)
    total = total + lax.dot_general(ones, low, dims, preferred_element_type=jnp.float32)
    return total[0:1, :]


def packed_pairs(pairs, location, slots, demo_count, share, part, reps, capacity, width):
    blocks = pairs.shape[0]
    own_blocks = blocks // reps
    names = lax.broadcasted_iota(jnp.int32, (blocks, 128), 1)
    places = lax.broadcasted_iota(jnp.int32, (blocks, width), 1)
    block = lax.broadcasted_iota(jnp.int32, (blocks, 1), 0)
    side_of = lax.div(block, jnp.int32(own_blocks))
    count = pairs[:, slots : slots + 1]
    mine, owners, locals_, chosen = [], [], [], []
    for s in range(slots):
        found = jnp.zeros((blocks, 128), jnp.int32)
        for k in range(location.shape[0]):
            hit = pairs[:, s : s + 1] - 128 * k == names
            found = found + jnp.where(hit, location[k : k + 1, :], 0)
        stored = jnp.sum(found, axis=1, keepdims=True)
        owner = lax.div(stored, jnp.int32(demo_count))
        local = stored - owner * demo_count
        side = lax.div(local, jnp.int32(share))
        use = (count > s) & (side == part)
        mine.append(jnp.where(use, 1, 0))
        owners.append(owner)
        locals_.append(local - side * share)
        chosen.append(jnp.where((owner == names) & use, 1, 0))
    in_row = sum(mine)
    of_owner = sum(chosen)
    rows_wide = lax.broadcasted_iota(jnp.int32, (blocks, 128), 0)
    in_wide = jnp.broadcast_to(in_row, (blocks, 128))
    before = jnp.zeros((blocks, 128), jnp.int32)
    running = jnp.zeros((blocks, 128), jnp.int32)
    for b in range(blocks - 1):
        after = rows_wide > b
        near = after & (rows_wide < (b // own_blocks + 1) * own_blocks)
        before = before + jnp.where(after, in_wide[b : b + 1, :], 0)
        running = running + jnp.where(near, of_owner[b : b + 1, :], 0)
    rank = before[:, 0:1]
    rows = [jnp.zeros((blocks, width), jnp.int32) for _ in range(5)]
    for s in range(slots):
        own_rank = jnp.sum(running * chosen[s], axis=1, keepdims=True)
        place = (owners[s] * reps + side_of) * capacity + own_rank
        hit = (rank == places) & (mine[s] > 0)
        at_place = (place == places) & (mine[s] > 0)
        values = (block, owners[s] * share + locals_[s], place, block - side_of * own_blocks, locals_[s])
        for k, value in enumerate(values):
            rows[k] = rows[k] + jnp.where(hit if k < 3 else at_place, value, 0)
        rank = rank + mine[s]
        running = running + chosen[s]
    total = jnp.broadcast_to(in_row, (blocks, width))
    rows = [rows[0], rows[1], total, rows[2], rows[3], rows[4]]
    return [jnp.sum(r, axis=0, keepdims=True) for r in rows]


def gather_kernel(n, reps, slots, *refs):
    demo, rollout, projection_hbm, pair_block, pair_count, location_hbm, costs, lists = refs[:8]
    hops = n // 4
    refs = list(refs[8:])
    own_slots, twin_slots = refs[: 2 * hops - 1], refs[2 * hops - 1 : 4 * hops - 1]
    refs = refs[4 * hops - 1 :]
    u_slots, norm_slots = refs[: reps - 1], refs[reps - 1 : 2 * (reps - 1)]
    row_terms = refs[2 * (reps - 1) : 3 * reps - 2]
    (demo_in, rollout_in, projection, location, block_in, count_in, own_pairs, own_v, own_vnorm, vnorm, own_u, own_unorm,
     pairs, known, ring_send, ring_recv, side_send, side_recv, norm_send, norm_recv, rep_send, rep_recv, home) = refs[3 * reps - 2 :]
    me = lax.axis_index("roll")
    part = lax.axis_index("rep")
    chips = n // 2
    core = lax.rem(me, 2)
    chip = me // 2
    odd = lax.rem(chip, 2)
    place = (1 - odd) * (chip // 2) + odd * (chips - 1 - chip // 2)

    def at_place(p):
        p = lax.rem(p + 2 * chips, chips)
        high = p // hops
        return ((1 - high) * (2 * p) + high * (2 * (chips - 1 - p) + 1)) * 2 + core

    twin = {"roll": me + 1 - 2 * core}
    ways = ({"roll": at_place(place + 1)}, {"roll": at_place(place - 1)})
    rows = own_v.shape[0] // CHUNKS
    feats = projection.shape[1]
    share, blk = own_vnorm.shape
    own_blocks = own_unorm.shape[0]
    capacity = max(1, own_blocks * slots // n)
    unit = SCALE / feats
    near = others("roll", n) + others("rep", reps)
    fetch_demo = pltpu.make_async_copy(demo.at[pl.ds(part * (share * blk), share * blk)], demo_in, home.at[0])
    fetch_demo.start()
    fetches = [
        pltpu.make_async_copy(source, target, home.at[2 + k])
        for k, (source, target) in enumerate((
            (projection_hbm, projection),
            (pair_block, block_in),
            (pair_count, count_in),
            (location_hbm, location),
        ))
    ]
    for fetch in fetches:
        fetch.start()
    fetch_rollout = pltpu.make_async_copy(rollout, rollout_in, home.at[1])
    fetch_rollout.start()
    barrier = pltpu.get_barrier_semaphore()
    for partner in near:
        pl.semaphore_signal(barrier, inc=1, device_id=partner, device_id_type=MESH)
    for fetch in fetches:
        fetch.wait()
    own_pairs[...] = jnp.zeros_like(own_pairs)
    own_pairs[0:slots, 0 : block_in.shape[1]] = block_in[...]
    own_pairs[slots : slots + 1, 0 : count_in.shape[1]] = count_in[...]
    turned = jnp.transpose(projection[...])
    fetch_demo.wait()
    for b in range(share):
        own_v[b] = lax.dot_general(
            turned, demo_in[b * blk : (b + 1) * blk, :], (((1,), (1,)), ((), ())),
            preferred_element_type=jnp.float32,
        ).astype(jnp.bfloat16)
    pl.semaphore_wait(barrier, len(near))

    def own_slot(way, s):
        if s == 0:
            return own_v
        return own_slots[2 * (hops - 1) if s == hops else way * (hops - 1) + s - 1]

    def twin_slot(way, s):
        if s == 0:
            return twin_slots[2 * hops - 1]
        return twin_slots[2 * (hops - 1) if s == hops else way * (hops - 1) + s - 1]

    def remote(source, target, sends, recvs, device):
        copy = pltpu.make_async_remote_copy(
            src_ref=source, dst_ref=target, send_sem=sends, recv_sem=recvs, device_id=device, device_id_type=MESH
        )
        copy.start()
        return copy

    def send(s, way, q):
        piece = pl.ds(q * rows, rows)
        return remote(
            own_slot(way, s).at[piece], own_slot(way, s + 1).at[piece],
            ring_send.at[way, s, q], ring_recv.at[way, s, q], ways[way],
        )

    crossing = {}

    def cross(s, way, q):
        piece = pl.ds(q * rows, rows)
        copy = remote(
            own_slot(way, s).at[piece], twin_slot(way, s).at[piece],
            side_send.at[way, s, q], side_recv.at[way, s, q], twin,
        )
        crossing.setdefault((0 if s == hops else way, s), []).append(copy)

    def travels(s, way, q):
        return s < hops - 1 or (s == hops - 1 and q * 2 // CHUNKS == way)

    moving = {}
    for q in range(CHUNKS):
        for way in range(2):
            if travels(0, way, q):
                moving[0, way, q] = send(0, way, q)

    def to_reps(source, targets, which):
        return [
            remote(source, targets[d], rep_send.at[which, d], rep_recv.at[which, d], partner)
            for d, partner in enumerate(others("rep", reps))
        ]

    pair_copies = to_reps(own_pairs, [pairs.at[part]] * (reps - 1), 0)
    pairs[part] = own_pairs[...]
    for q in range(CHUNKS):
        cross(0, 0, q)
    fetch_rollout.wait()

    def do_rollout(b, carry):
        rows_b = pl.ds(pl.multiple_of(b * blk, blk), blk)
        codes = jnp.dot(
            rollout_in[rows_b, :], projection[...], preferred_element_type=jnp.float32
        ).astype(jnp.bfloat16)
        own_u[b] = codes
        own_unorm[pl.ds(b, 1), :] = block_norms(codes)
        return carry

    lax.fori_loop(0, own_blocks, do_rollout, 0)
    frame_copies = to_reps(own_u, u_slots, 2) + to_reps(own_unorm, norm_slots, 1)

    def do_demo(b, carry):
        wide = own_v[b].astype(jnp.float32)
        own_vnorm[pl.ds(b, 1), :] = jnp.sum(wide * wide, axis=0, keepdims=True)
        return carry

    lax.fori_loop(0, share, do_demo, 0)
    vnorm_copies = [
        remote(own_vnorm, vnorm.at[me], norm_send.at[d], norm_recv.at[d], partner)
        for d, partner in enumerate(others("roll", n))
    ]
    vnorm[me] = own_vnorm[...]

    def spread_norms(source, target):
        def one(b, carry):
            line = source[pl.ds(b, 1), :] * (-unit)
            target[b] = jnp.transpose(jnp.broadcast_to(line, (blk, blk)))
            return carry

        lax.fori_loop(0, own_blocks, one, 0, unroll=4)

    spread_norms(own_unorm, row_terms[0])
    for copy in pair_copies:
        copy.wait()
    square = [
        jnp.concatenate([pairs[r], jnp.zeros((128 - pairs.shape[1], 128), jnp.int32)], axis=0)
        for r in range(reps)
    ]
    everyone = jnp.concatenate([jnp.transpose(a)[0:own_blocks, :] for a in square], axis=0)
    found = packed_pairs(
        everyone, location[...], slots, share * reps, share, part, reps, capacity, lists.shape[1]
    )
    lists[...] = jnp.zeros_like(lists)
    for k, row in enumerate(found):
        lists[k : k + 1, :] = row
    to_scalars = pltpu.make_async_copy(lists, known, home.at[6])
    to_scalars.start()
    to_scalars.wait()
    for copy in vnorm_copies:
        copy.wait_recv()

    met = set()

    def work(way, s, far_side, other):
        slot = (twin_slot if far_side else own_slot)(way, s)
        owner = at_place(place - s) if way == 0 else at_place(place + s)
        if far_side:
            owner = owner + 1 - 2 * core
            if (way, s) not in met:
                met.add((way, s))
                for copy in crossing[way, s]:
                    copy.wait_recv()
        if other and other not in met:
            met.add(other)
            for copy in frame_copies[other - 1 :: reps - 1]:
                copy.wait_recv()
            spread_norms(norm_slots[other - 1], row_terms[other])
        codes = u_slots[other - 1] if other else own_u
        rep = lax.rem(part - other + reps, reps)
        first = (owner * reps + rep) * capacity

        def tile(k, carry):
            at = first + k
            b = known[4, at]
            t = known[5, at]
            crossed = jnp.dot(codes[b], slot[t], preferred_element_type=jnp.float32)
            costs[pl.ds(pl.multiple_of(at * blk, blk), blk), :] = (
                crossed * (2.0 * unit) + row_terms[other][b] + vnorm[owner, t].reshape(1, blk) * (-unit)
            )
            return carry

        lax.fori_loop(0, capacity, tile, 0, unroll=min(4, capacity))

    queue, later = [], []

    def ready(s):
        for far_side in (False, True):
            for way in range(1 if s in (0, hops) else 2):
                queue.append((way, s, far_side, 0))
                for other in range(1, reps):
                    (later if s < 2 else queue).append((way, s, far_side, other))

    def run(most):
        for _ in range(min(most, len(queue))):
            work(*queue.pop(0))

    ready(0)
    run(1)
    for s in range(1, hops + 1):
        if s == hops - 1:
            queue[:0] = later
        half = CHUNKS // 2
        order = range(CHUNKS) if s < hops else [q // 2 + half * (q % 2) for q in range(CHUNKS)]
        for q in order:
            for way in range(2):
                if (s - 1, way, q) not in moving:
                    continue
                moving[s - 1, way, q].wait_recv()
                if travels(s, way, q):
                    moving[s, way, q] = send(s, way, q)
                cross(s, way, q)
            run(4 if s < hops else 2)
        ready(s)
    run(len(queue))
    for copy in moving.values():
        copy.wait_send()
    for copies in crossing.values():
        for copy in copies:
            copy.wait_send()
    for copy in frame_copies + vnorm_copies:
        copy.wait_send()


def gathered(n, reps, demo, rollout, projection, pair_block, pair_count, location):
    hops = n // 4
    own_blocks, slots = pair_block.shape
    blk = rollout.shape[0] // own_blocks
    feats = projection.shape[1]
    share = demo.shape[0] // blk // reps
    places = n * reps * max(1, own_blocks * slots // n)
    location = location.reshape(-1, 128)
    own_pairs = (slots // 8 * 8 + 8, 128)
    hbm = pl.BlockSpec(memory_space=pltpu.HBM)
    vmem = pl.BlockSpec(memory_space=pltpu.VMEM)
    dma = pltpu.SemaphoreType.DMA
    wide, code = jnp.float32, jnp.bfloat16
    slot = pltpu.VMEM((share, feats, blk), code)
    frames = pltpu.VMEM((own_blocks, blk, feats), code)
    scratch = [slot] * (4 * hops - 1) + [frames] * (reps - 1) + [pltpu.VMEM((own_blocks, blk), wide)] * (reps - 1)
    scratch += [pltpu.VMEM((own_blocks, blk, blk), wide)] * reps
    scratch += [
        pltpu.VMEM((share * blk, feats), code),
        pltpu.VMEM(rollout.shape, code),
        pltpu.VMEM(projection.shape, code),
        pltpu.VMEM(location.shape, jnp.int32),
        pltpu.VMEM((slots, own_blocks), jnp.int32),
        pltpu.VMEM((1, own_blocks), jnp.int32),
        pltpu.VMEM(own_pairs, jnp.int32),
        slot,
        pltpu.VMEM((share, blk), wide),
        pltpu.VMEM((n, share, blk), wide),
        frames,
        pltpu.VMEM((own_blocks, blk), wide),
        pltpu.VMEM((reps,) + own_pairs, jnp.int32),
    ]
    held = sum(math.prod(a.shape) * a.dtype.itemsize for a in scratch)
    lists = jax.ShapeDtypeStruct((8, places + 128), jnp.int32)
    scratch += [
        pltpu.SMEM(lists.shape, jnp.int32),
        dma((2, hops, CHUNKS)), dma((2, hops, CHUNKS)),
        dma((2, hops + 1, CHUNKS)), dma((2, hops + 1, CHUNKS)),
        dma((n - 1,)), dma((n - 1,)),
        dma((3, reps - 1)), dma((3, reps - 1)),
        dma((7,)),
    ]
    return pl.pallas_call(
        functools.partial(gather_kernel, n, reps, slots),
        out_shape=[jax.ShapeDtypeStruct((places * blk, blk), wide), lists],
        in_specs=[hbm] * 6,
        out_specs=[vmem] * 2,
        scratch_shapes=scratch,
        compiler_params=pltpu.CompilerParams(
            collective_id=0, has_side_effects=True, vmem_limit_bytes=held + 3 * MIB
        ),
        name="gather_costs",
    )(*(
        pltpu.with_memory_space_constraint(a, pltpu.HBM)
        for a in (demo, rollout, projection, pair_block.T, pair_count[None, :], location)
    ))


def column_kernel(n, reps, sums, *refs):
    if reps:
        out, both, landed, full, held, first_send, first_recv, second_send, second_recv, rep_send, rep_recv = refs
    else:
        out, landed, full, first_send, first_recv, second_send, second_recv = refs
    me = lax.axis_index("roll")
    partners = others("roll", n)
    twins = others("rep", reps) if reps else []
    greet(partners + twins)
    copies = []
    for d, partner in enumerate(partners):
        copy = pltpu.make_async_remote_copy(
            src_ref=sums.at[partner["roll"]], dst_ref=landed.at[d],
            send_sem=first_send.at[d], recv_sem=first_recv.at[d],
            device_id=partner, device_id_type=MESH,
        )
        copy.start()
        copies.append(copy)
    total = sums[me]
    for d, copy in enumerate(copies):
        copy.wait_recv()
        total = total + landed[d]
    pot = SHIFT - jnp.log2(total + FLOOR)
    full[me] = pot
    seconds = []
    for d, partner in enumerate(partners):
        copy = pltpu.make_async_remote_copy(
            src_ref=full.at[me], dst_ref=full.at[me],
            send_sem=second_send.at[d], recv_sem=second_recv.at[d],
            device_id=partner, device_id_type=MESH,
        )
        copy.start()
        seconds.append(copy)
    if reps:
        part = lax.axis_index("rep")
        held[part] = pot * (1.0 / SCALE)
        for d, partner in enumerate(twins):
            copy = pltpu.make_async_remote_copy(
                src_ref=held.at[part], dst_ref=held.at[part],
                send_sem=rep_send.at[d], recv_sem=rep_recv.at[d],
                device_id=partner, device_id_type=MESH,
            )
            copy.start()
            seconds.append(copy)
    for copy in copies:
        copy.wait_send()
    for copy in seconds:
        copy.wait()
    out[...] = full[...]
    if reps:
        both[...] = held[...]


def column_potentials(n, reps, sums, call):
    last = call == ITERS - 1
    share, blk = sums.shape[0] // n, sums.shape[1]
    if n > DIRECT:
        pot = SHIFT - jnp.log2(lax.psum(sums, "roll") + FLOOR)
        if not last:
            return pot, None
        mine = lax.dynamic_slice_in_dim(pot, lax.axis_index("roll") * share, share, 0)
        return pot, lax.all_gather(mine, "rep") / SCALE
    sums = sums.reshape(n, share, blk)
    dma = pltpu.SemaphoreType.DMA
    vmem = pl.BlockSpec(memory_space=pltpu.VMEM)
    both = (reps, share, blk)
    outs = [jax.ShapeDtypeStruct(sums.shape, sums.dtype)]
    scratch = [pltpu.VMEM((n - 1, share, blk), jnp.float32), pltpu.VMEM((n, share, blk), jnp.float32)]
    if last:
        outs.append(jax.ShapeDtypeStruct(both, sums.dtype))
        scratch.append(pltpu.VMEM(both, jnp.float32))
    scratch += [dma((n - 1,))] * 4
    if last:
        scratch += [dma((reps - 1,))] * 2
    out = pl.pallas_call(
        functools.partial(column_kernel, n, reps if last else 0),
        out_shape=outs,
        in_specs=[vmem],
        out_specs=[vmem] * len(outs),
        scratch_shapes=scratch,
        compiler_params=pltpu.CompilerParams(
            collective_id=1 + call, has_side_effects=True, vmem_limit_bytes=MIB
        ),
        name="column_exchange_%d" % call,
    )(sums)
    return out[0].reshape(n * share, blk), out[1] if last else None


def row_kernel(reps, last, sums, *refs):
    outs, (landed, send_sem, recv_sem) = refs[:-3], refs[-3:]
    part = lax.axis_index("rep")
    partners = others("rep", reps)
    greet(partners)
    copies = []
    for d, partner in enumerate(partners):
        copy = pltpu.make_async_remote_copy(
            src_ref=sums, dst_ref=landed.at[d], send_sem=send_sem.at[d], recv_sem=recv_sem.at[d],
            device_id=partner, device_id_type=MESH,
        )
        copy.start()
        copies.append(copy)
    for copy in copies:
        copy.wait_recv()
    if last:
        heights, weighted = (
            sum((landed[d, k, part] for d in range(reps - 1)), sums[k, part]) for k in range(2)
        )
        heights = heights + FLOOR
        outs[0][...] = -(weighted + UNMATCHED * FLOOR) / heights
        outs[1][...] = (SHIFT - jnp.log2(heights)) * (1.0 / SCALE)
    else:
        total = sum((landed[d, 0] for d in range(reps - 1)), sums[0])
        outs[0][...] = SHIFT - jnp.log2(total + FLOOR)
    for copy in copies:
        copy.wait_send()


def row_totals(reps, sums, call):
    last = call == ITERS - 1
    sums = sums.reshape(sums.shape[0], reps, -1, sums.shape[2])
    dma = pltpu.SemaphoreType.DMA((reps - 1,))
    vmem = pl.BlockSpec(memory_space=pltpu.VMEM)
    shapes = [sums.shape[2:]] * 2 if last else [sums.shape[1:]]
    return pl.pallas_call(
        functools.partial(row_kernel, reps, last),
        out_shape=[jax.ShapeDtypeStruct(shape, sums.dtype) for shape in shapes],
        in_specs=[vmem],
        out_specs=[vmem] * len(shapes),
        scratch_shapes=[pltpu.VMEM((reps - 1,) + sums.shape, jnp.float32), dma, dma],
        compiler_params=pltpu.CompilerParams(
            collective_id=1 + ITERS + call, has_side_effects=True, vmem_limit_bytes=2 * MIB
        ),
        name="row_exchange_%d" % call,
    )(sums)


def body(rollout, demo, projection, location, pair_block, pair_count):
    own_blocks = pair_block.shape[0]
    blk = rollout.shape[0] // own_blocks
    n = lax.axis_size("roll")
    reps = lax.axis_size("rep")
    demo_count = demo.shape[0] // blk
    share = demo_count // reps
    sizes = (reps * own_blocks, n * share, blk)
    stored = n <= DIRECT
    if stored:
        costs, lists = gathered(n, reps, demo, rollout, projection, pair_block, pair_count, location)
        data = (costs,)
    else:
        part = lax.axis_index("rep")
        own_demo = lax.dynamic_slice_in_dim(demo, part * (share * blk), share * blk, 0)
        own_v = project(own_demo, projection)
        own_u = project(rollout, projection)
        flipped = own_v.reshape(share, blk, -1).transpose(0, 2, 1).reshape(-1, blk)
        v, vnorm = (lax.all_gather(a, "roll") for a in (flipped, norms(own_v, blk)))
        u, unorm = (lax.all_gather(a, "rep") for a in (own_u, norms(own_u, blk)))
        pairs, counts = (lax.all_gather(a, "rep", tiled=True) for a in (pair_block, pair_count))
        lists = listed(pairs, counts, location, demo_count, share, part)
        data = tuple(a.reshape(-1, a.shape[-1]) for a in (u, v, unorm, vnorm))

    roll_pot = None
    for iteration in range(ITERS):
        sums = run_pass("column", sizes, lists, data, roll_pot, stored)[0]
        demo_pot, held_pot = column_potentials(n, reps, sums, iteration)
        kind = "final" if iteration == ITERS - 1 else "row"
        sums = run_pass(kind, sizes, lists, data, demo_pot, stored)[0]
        results = row_totals(reps, sums, iteration)
        roll_pot = results[0].reshape(-1, blk) if kind == "row" else None
    return results[0].reshape(-1), results[1].reshape(-1), held_pot.reshape(-1)


def solution(mesh):
    placed = (
        P(("roll", "rep"), None),
        P("roll", None),
        P(),
        P(),
        P(("roll", "rep"), None),
        P(("roll", "rep")),
    )
    return jax.shard_map(
        body,
        mesh=mesh,
        in_specs=placed,
        out_specs=(P(("roll", "rep")), P(("roll", "rep")), P("roll")),
        check_vma=False,
    )
```

```python
import functools
import math

import jax
import jax.numpy as jnp
from jax import lax
from jax.experimental import pallas as pl
from jax.experimental.pallas import tpu as pltpu
from jax.sharding import PartitionSpec as P

ITERS = 2
EPSILON = 0.02
UNMATCHED = 2.0
SLACK = -100.0
LOG2E = math.log2(math.e)
SCALE = LOG2E / EPSILON
SHIFT = 50.0 * LOG2E
FLOOR = math.exp(SLACK + 50.0)
UNROLL = 4
DIRECT = 16
CHUNKS = 4
MIB = 1024 * 1024
MESH = pl.DeviceIdType.MESH


def pass_kernel(kind, fresh, stored, lists_ref, *refs):
    refs = list(refs)
    if stored:
        kept = refs.pop(0)
    else:
        u_ref, v_ref, unorm_ref, vnorm_ref = refs[:4]
        refs = refs[4:]
    pot_ref = None if fresh else refs.pop(0)
    out_ref = refs.pop(0)
    sums_ref = refs.pop()
    if kind == "final":
        wsums_ref = refs.pop()
        wsums_ref[...] = jnp.zeros_like(wsums_ref)
    sums_ref[...] = jnp.zeros_like(sums_ref)
    blk = out_ref.shape[-1]
    by_column = kind == "column"
    roll_blocks = (refs[0] if refs else sums_ref).shape[0] // blk

    if not stored:
        row_norm = refs.pop(0)
        feats = u_ref.shape[1]
        unit = SCALE / feats
        roll_blocks = unorm_ref.shape[0]

    def spread(source, factor, target):
        def one(b, carry):
            line = source[pl.ds(b, 1), :] * factor
            rows = pl.ds(pl.multiple_of(b * blk, blk), blk)
            target[rows, :] = jnp.transpose(jnp.broadcast_to(line, (blk, blk)))
            return carry

        lax.fori_loop(0, roll_blocks, one, 0, unroll=8)

    if not stored:
        spread(unorm_ref, -unit, row_norm)
    if by_column and not fresh:
        row_pot = refs.pop(0)
        spread(pot_ref, 1.0, row_pot)

    total = lists_ref[2, 0]

    def step(k, carry):
        parts = []
        for p in range(UNROLL):
            at = k * UNROLL + p
            b = lists_ref[0, at]
            t = lists_ref[1, at]
            live = jnp.where(at < total, SHIFT, -1e30)
            rows = pl.ds(pl.multiple_of(b * blk, blk), blk)
            if stored:
                y = kept[pl.ds(pl.multiple_of(lists_ref[3, at] * blk, blk), blk), :]
            else:
                crossed = lax.dot_general(
                    u_ref[rows, :],
                    v_ref[pl.ds(pl.multiple_of(t * feats, feats), feats), :],
                    (((1,), (0,)), ((), ())),
                    preferred_element_type=jnp.float32,
                )
                y = crossed * (2.0 * unit) + row_norm[rows, :] + vnorm_ref[pl.ds(t, 1), :] * (-unit)
            if by_column:
                x = y + live if fresh else y + row_pot[rows, :] + live
                parts.append((t, jnp.sum(jnp.exp2(x).reshape(blk // 8, 8, blk), axis=0)))
            else:
                e = jnp.exp2(y + (pot_ref[pl.ds(t, 1), :] + live))
                parts.append((rows, e, e * y if kind == "final" else None))
        for where, e, *weighted in parts:
            if by_column:
                at8 = pl.ds(pl.multiple_of(where * 8, 8), 8)
                sums_ref[at8, :] = sums_ref[at8, :] + e
            else:
                sums_ref[where, :] = sums_ref[where, :] + e
                if kind == "final":
                    wsums_ref[where, :] = wsums_ref[where, :] + weighted[0]
        return carry

    lax.fori_loop(0, (total + UNROLL - 1) // UNROLL, step, 0)

    if by_column:
        out_ref[...] = jnp.sum(sums_ref[...].reshape(out_ref.shape[0], 8, blk), axis=1)
    else:

        def finish(b, carry):
            rows = pl.ds(pl.multiple_of(b * blk, blk), blk)
            out_ref[0, pl.ds(b, 1), :] = jnp.sum(jnp.transpose(sums_ref[rows, :]), axis=0, keepdims=True)
            if kind == "final":
                out_ref[1, pl.ds(b, 1), :] = jnp.sum(
                    jnp.transpose(wsums_ref[rows, :]), axis=0, keepdims=True
                ) * (-1.0 / SCALE)
            return carry

        lax.fori_loop(0, roll_blocks, finish, 0, unroll=8)


def run_pass(kind, sizes, lists, data, pot, stored):
    fresh = pot is None
    roll_blocks, targets, blk = sizes
    pairs = lists.shape[1] - 128
    smem = pl.BlockSpec(memory_space=pltpu.SMEM)
    vmem = pl.BlockSpec(memory_space=pltpu.VMEM)
    frames = pltpu.VMEM((roll_blocks * blk, blk), jnp.float32)
    by_column = kind == "column"
    args = list(data)
    if not fresh:
        args.append(pot)
    if by_column:
        outs = [jax.ShapeDtypeStruct((targets, blk), jnp.float32)]
        sums = [pltpu.VMEM((targets * 8, blk), jnp.float32)]
    else:
        outs = [jax.ShapeDtypeStruct((2 if kind == "final" else 1, roll_blocks, blk), jnp.float32)]
        sums = [frames] * (2 if kind == "final" else 1)
    scratch = ([] if stored else [frames]) + ([frames] if by_column and not fresh else []) + sums
    held = sum(math.prod(a.shape) * a.dtype.itemsize for a in scratch + ([] if stored else args + outs))
    return pl.pallas_call(
        functools.partial(pass_kernel, kind, fresh, stored),
        out_shape=outs,
        in_specs=[smem] + [vmem] * len(args),
        out_specs=[vmem] * len(outs),
        scratch_shapes=scratch,
        compiler_params=pltpu.CompilerParams(vmem_limit_bytes=held + 2 * MIB),
        cost_estimate=pl.CostEstimate(
            flops=pairs * blk * blk * (4 if stored else data[0].shape[1]),
            bytes_accessed=pairs * blk * blk * 4,
            transcendentals=pairs * blk * blk // 2,
        ),
        name="pass_" + kind,
    )(lists, *args)


def listed(pair_block, pair_count, location, demo_count, share, part):
    roll_blocks, slots = pair_block.shape
    n = roll_blocks * slots
    names = jnp.arange(location.shape[0], dtype=jnp.int32)
    flat = pair_block.reshape(n)
    stored = jnp.sum(jnp.where(flat[:, None] == names[None, :], location[None, :], 0), axis=1)
    active = (jnp.arange(slots, dtype=jnp.int32)[None, :] < pair_count[:, None]).reshape(n)
    local = stored % demo_count
    mine = active & (local // share == part)
    target = (stored // demo_count) * share + local % share
    ids = jnp.arange(n, dtype=jnp.int32)
    rank = jnp.sum((mine[None, :] & (ids[None, :] < ids[:, None])).astype(jnp.int32), axis=1)
    place = jnp.where(mine, rank, -1)
    hit = place[None, :] == ids[:, None]
    home = jnp.sum(jnp.where(hit, (ids // slots)[None, :], 0), axis=1)
    target = jnp.sum(jnp.where(hit, target[None, :], 0), axis=1)
    total = jnp.sum(mine.astype(jnp.int32)).reshape(1)
    lists = jnp.stack([home, target, jnp.broadcast_to(total, (n,))])
    return jnp.pad(lists, ((0, 0), (0, 128)))


def project(frames, projection):
    return jnp.dot(frames, projection, preferred_element_type=jnp.float32).astype(jnp.bfloat16)


def norms(codes, blk):
    wide = codes.astype(jnp.float32)
    return jnp.sum(wide * wide, axis=1).reshape(-1, blk)


def greet(partners):
    barrier = pltpu.get_barrier_semaphore()
    for partner in partners:
        pl.semaphore_signal(barrier, inc=1, device_id=partner, device_id_type=MESH)
    pl.semaphore_wait(barrier, len(partners))


def others(axis, size):
    me = lax.axis_index(axis)
    return [{axis: lax.rem(me + d, size)} for d in range(1, size)]


def block_norms(codes):
    wide = codes.astype(jnp.float32)
    square = wide * wide
    high = square.astype(jnp.bfloat16)
    low = (square - high.astype(jnp.float32)).astype(jnp.bfloat16)
    ones = jnp.ones((8, codes.shape[1]), jnp.bfloat16)
    dims = (((1,), (1,)), ((), ()))
    total = lax.dot_general(ones, high, dims, preferred_element_type=jnp.float32)
    total = total + lax.dot_general(ones, low, dims, preferred_element_type=jnp.float32)
    return total[0:1, :]


def packed_pairs(pairs, location, slots, demo_count, share, part, reps, capacity, width):
    blocks = pairs.shape[0]
    own_blocks = blocks // reps
    names = lax.broadcasted_iota(jnp.int32, (blocks, 128), 1)
    places = lax.broadcasted_iota(jnp.int32, (blocks, width), 1)
    block = lax.broadcasted_iota(jnp.int32, (blocks, 1), 0)
    side_of = lax.div(block, jnp.int32(own_blocks))
    count = pairs[:, slots : slots + 1]
    mine, owners, locals_, chosen = [], [], [], []
    for s in range(slots):
        found = jnp.zeros((blocks, 128), jnp.int32)
        for k in range(location.shape[0]):
            hit = pairs[:, s : s + 1] - 128 * k == names
            found = found + jnp.where(hit, location[k : k + 1, :], 0)
        stored = jnp.sum(found, axis=1, keepdims=True)
        owner = lax.div(stored, jnp.int32(demo_count))
        local = stored - owner * demo_count
        side = lax.div(local, jnp.int32(share))
        use = (count > s) & (side == part)
        mine.append(jnp.where(use, 1, 0))
        owners.append(owner)
        locals_.append(local - side * share)
        chosen.append(jnp.where((owner == names) & use, 1, 0))
    in_row = sum(mine)
    of_owner = sum(chosen)
    rows_wide = lax.broadcasted_iota(jnp.int32, (blocks, 128), 0)
    in_wide = jnp.broadcast_to(in_row, (blocks, 128))
    before = jnp.zeros((blocks, 128), jnp.int32)
    running = jnp.zeros((blocks, 128), jnp.int32)
    for b in range(blocks - 1):
        after = rows_wide > b
        near = after & (rows_wide < (b // own_blocks + 1) * own_blocks)
        before = before + jnp.where(after, in_wide[b : b + 1, :], 0)
        running = running + jnp.where(near, of_owner[b : b + 1, :], 0)
    rank = before[:, 0:1]
    rows = [jnp.zeros((blocks, width), jnp.int32) for _ in range(5)]
    for s in range(slots):
        own_rank = jnp.sum(running * chosen[s], axis=1, keepdims=True)
        place = (owners[s] * reps + side_of) * capacity + own_rank
        hit = (rank == places) & (mine[s] > 0)
        at_place = (place == places) & (mine[s] > 0)
        values = (block, owners[s] * share + locals_[s], place, block - side_of * own_blocks, locals_[s])
        for k, value in enumerate(values):
            rows[k] = rows[k] + jnp.where(hit if k < 3 else at_place, value, 0)
        rank = rank + mine[s]
        running = running + chosen[s]
    total = jnp.broadcast_to(in_row, (blocks, width))
    rows = [rows[0], rows[1], total, rows[2], rows[3], rows[4]]
    return [jnp.sum(r, axis=0, keepdims=True) for r in rows]


def gather_kernel(n, reps, slots, *refs):
    demo, rollout, projection_hbm, pair_block, pair_count, location_hbm, costs, lists = refs[:8]
    hops = n // 4
    refs = list(refs[8:])
    own_slots, twin_slots = refs[: 2 * hops - 1], refs[2 * hops - 1 : 4 * hops - 1]
    refs = refs[4 * hops - 1 :]
    u_slots, norm_slots = refs[: reps - 1], refs[reps - 1 : 2 * (reps - 1)]
    row_terms = refs[2 * (reps - 1) : 3 * reps - 2]
    (demo_in, rollout_in, projection, location, block_in, count_in, own_pairs, own_v, own_vnorm, vnorm, own_u, own_unorm,
     pairs, known, ring_send, ring_recv, side_send, side_recv, norm_send, norm_recv, rep_send, rep_recv, home) = refs[3 * reps - 2 :]
    me = lax.axis_index("roll")
    part = lax.axis_index("rep")
    chips = n // 2
    core = lax.rem(me, 2)
    chip = me // 2
    odd = lax.rem(chip, 2)
    place = (1 - odd) * (chip // 2) + odd * (chips - 1 - chip // 2)

    def at_place(p):
        p = lax.rem(p + 2 * chips, chips)
        high = p // hops
        return ((1 - high) * (2 * p) + high * (2 * (chips - 1 - p) + 1)) * 2 + core

    twin = {"roll": me + 1 - 2 * core}
    ways = ({"roll": at_place(place + 1)}, {"roll": at_place(place - 1)})
    rows = own_v.shape[0] // CHUNKS
    feats = projection.shape[1]
    share, blk = own_vnorm.shape
    own_blocks = own_unorm.shape[0]
    capacity = max(1, own_blocks * slots // n)
    unit = SCALE / feats
    near = others("roll", n) + others("rep", reps)
    fetch_demo = pltpu.make_async_copy(demo.at[pl.ds(part * (share * blk), share * blk)], demo_in, home.at[0])
    fetch_demo.start()
    fetches = [
        pltpu.make_async_copy(source, target, home.at[2 + k])
        for k, (source, target) in enumerate((
            (projection_hbm, projection),
            (pair_block, block_in),
            (pair_count, count_in),
            (location_hbm, location),
        ))
    ]
    for fetch in fetches:
        fetch.start()
    fetch_rollout = pltpu.make_async_copy(rollout, rollout_in, home.at[1])
    fetch_rollout.start()
    barrier = pltpu.get_barrier_semaphore()
    for partner in near:
        pl.semaphore_signal(barrier, inc=1, device_id=partner, device_id_type=MESH)
    for fetch in fetches:
        fetch.wait()
    own_pairs[...] = jnp.zeros_like(own_pairs)
    own_pairs[0:slots, 0 : block_in.shape[1]] = block_in[...]
    own_pairs[slots : slots + 1, 0 : count_in.shape[1]] = count_in[...]
    turned = jnp.transpose(projection[...])
    fetch_demo.wait()
    for b in range(share):
        own_v[b] = lax.dot_general(
            turned, demo_in[b * blk : (b + 1) * blk, :], (((1,), (1,)), ((), ())),
            preferred_element_type=jnp.float32,
        ).astype(jnp.bfloat16)
    pl.semaphore_wait(barrier, len(near))

    def own_slot(way, s):
        if s == 0:
            return own_v
        return own_slots[2 * (hops - 1) if s == hops else way * (hops - 1) + s - 1]

    def twin_slot(way, s):
        if s == 0:
            return twin_slots[2 * hops - 1]
        return twin_slots[2 * (hops - 1) if s == hops else way * (hops - 1) + s - 1]

    def remote(source, target, sends, recvs, device):
        copy = pltpu.make_async_remote_copy(
            src_ref=source, dst_ref=target, send_sem=sends, recv_sem=recvs, device_id=device, device_id_type=MESH
        )
        copy.start()
        return copy

    def send(s, way, q):
        piece = pl.ds(q * rows, rows)
        return remote(
            own_slot(way, s).at[piece], own_slot(way, s + 1).at[piece],
            ring_send.at[way, s, q], ring_recv.at[way, s, q], ways[way],
        )

    crossing = {}

    def cross(s, way, q):
        piece = pl.ds(q * rows, rows)
        copy = remote(
            own_slot(way, s).at[piece], twin_slot(way, s).at[piece],
            side_send.at[way, s, q], side_recv.at[way, s, q], twin,
        )
        crossing.setdefault((0 if s == hops else way, s), []).append(copy)

    def travels(s, way, q):
        return s < hops - 1 or (s == hops - 1 and q * 2 // CHUNKS == way)

    moving = {}
    for q in range(CHUNKS):
        for way in range(2):
            if travels(0, way, q):
                moving[0, way, q] = send(0, way, q)

    def to_reps(source, targets, which):
        return [
            remote(source, targets[d], rep_send.at[which, d], rep_recv.at[which, d], partner)
            for d, partner in enumerate(others("rep", reps))
        ]

    pair_copies = to_reps(own_pairs, [pairs.at[part]] * (reps - 1), 0)
    pairs[part] = own_pairs[...]
    for q in range(CHUNKS):
        cross(0, 0, q)
    fetch_rollout.wait()

    def do_rollout(b, carry):
        rows_b = pl.ds(pl.multiple_of(b * blk, blk), blk)
        codes = jnp.dot(
            rollout_in[rows_b, :], projection[...], preferred_element_type=jnp.float32
        ).astype(jnp.bfloat16)
        own_u[b] = codes
        own_unorm[pl.ds(b, 1), :] = block_norms(codes)
        return carry

    lax.fori_loop(0, own_blocks, do_rollout, 0)
    frame_copies = to_reps(own_u, u_slots, 2) + to_reps(own_unorm, norm_slots, 1)

    def do_demo(b, carry):
        wide = own_v[b].astype(jnp.float32)
        own_vnorm[pl.ds(b, 1), :] = jnp.sum(wide * wide, axis=0, keepdims=True)
        return carry

    lax.fori_loop(0, share, do_demo, 0)
    vnorm_copies = [
        remote(own_vnorm, vnorm.at[me], norm_send.at[d], norm_recv.at[d], partner)
        for d, partner in enumerate(others("roll", n))
    ]
    vnorm[me] = own_vnorm[...]

    def spread_norms(source, target):
        def one(b, carry):
            line = source[pl.ds(b, 1), :] * (-unit)
            target[b] = jnp.transpose(jnp.broadcast_to(line, (blk, blk)))
            return carry

        lax.fori_loop(0, own_blocks, one, 0, unroll=4)

    spread_norms(own_unorm, row_terms[0])
    for copy in pair_copies:
        copy.wait()
    square = [
        jnp.concatenate([pairs[r], jnp.zeros((128 - pairs.shape[1], 128), jnp.int32)], axis=0)
        for r in range(reps)
    ]
    everyone = jnp.concatenate([jnp.transpose(a)[0:own_blocks, :] for a in square], axis=0)
    found = packed_pairs(
        everyone, location[...], slots, share * reps, share, part, reps, capacity, lists.shape[1]
    )
    lists[...] = jnp.zeros_like(lists)
    for k, row in enumerate(found):
        lists[k : k + 1, :] = row
    to_scalars = pltpu.make_async_copy(lists, known, home.at[6])
    to_scalars.start()
    to_scalars.wait()
    for copy in vnorm_copies:
        copy.wait_recv()

    met = set()

    def work(way, s, far_side, other):
        slot = (twin_slot if far_side else own_slot)(way, s)
        owner = at_place(place - s) if way == 0 else at_place(place + s)
        if far_side:
            owner = owner + 1 - 2 * core
            if (way, s) not in met:
                met.add((way, s))
                for copy in crossing[way, s]:
                    copy.wait_recv()
        if other and other not in met:
            met.add(other)
            for copy in frame_copies[other - 1 :: reps - 1]:
                copy.wait_recv()
            spread_norms(norm_slots[other - 1], row_terms[other])
        codes = u_slots[other - 1] if other else own_u
        rep = lax.rem(part - other + reps, reps)
        first = (owner * reps + rep) * capacity

        def tile(k, carry):
            at = first + k
            b = known[4, at]
            t = known[5, at]
            crossed = jnp.dot(codes[b], slot[t], preferred_element_type=jnp.float32)
            costs[pl.ds(pl.multiple_of(at * blk, blk), blk), :] = (
                crossed * (2.0 * unit) + row_terms[other][b] + vnorm[owner, t].reshape(1, blk) * (-unit)
            )
            return carry

        lax.fori_loop(0, capacity, tile, 0, unroll=min(8 if s == hops else 4, capacity))

    queue, later = [], []

    def ready(s):
        for far_side in (False, True):
            for way in range(1 if s in (0, hops) else 2):
                queue.append((way, s, far_side, 0))
                for other in range(1, reps):
                    (later if s < 2 else queue).append((way, s, far_side, other))

    def run(most):
        for _ in range(min(most, len(queue))):
            work(*queue.pop(0))

    ready(0)
    run(1)
    for s in range(1, hops + 1):
        if s == hops - 1:
            queue[:0] = later
        half = CHUNKS // 2
        order = range(CHUNKS) if s < hops else [q // 2 + half * (q % 2) for q in range(CHUNKS)]
        for q in order:
            for way in range(2):
                if (s - 1, way, q) not in moving:
                    continue
                moving[s - 1, way, q].wait_recv()
                if travels(s, way, q):
                    moving[s, way, q] = send(s, way, q)
                cross(s, way, q)
            run(4 if s < hops else 3 if q % half == 0 else 0)
        ready(s)
    run(len(queue))
    for copy in moving.values():
        copy.wait_send()
    for copies in crossing.values():
        for copy in copies:
            copy.wait_send()
    for copy in frame_copies + vnorm_copies:
        copy.wait_send()


def gathered(n, reps, demo, rollout, projection, pair_block, pair_count, location):
    hops = n // 4
    own_blocks, slots = pair_block.shape
    blk = rollout.shape[0] // own_blocks
    feats = projection.shape[1]
    share = demo.shape[0] // blk // reps
    places = n * reps * max(1, own_blocks * slots // n)
    location = location.reshape(-1, 128)
    own_pairs = (slots // 8 * 8 + 8, 128)
    hbm = pl.BlockSpec(memory_space=pltpu.HBM)
    vmem = pl.BlockSpec(memory_space=pltpu.VMEM)
    dma = pltpu.SemaphoreType.DMA
    wide, code = jnp.float32, jnp.bfloat16
    slot = pltpu.VMEM((share, feats, blk), code)
    frames = pltpu.VMEM((own_blocks, blk, feats), code)
    scratch = [slot] * (4 * hops - 1) + [frames] * (reps - 1) + [pltpu.VMEM((own_blocks, blk), wide)] * (reps - 1)
    scratch += [pltpu.VMEM((own_blocks, blk, blk), wide)] * reps
    scratch += [
        pltpu.VMEM((share * blk, feats), code),
        pltpu.VMEM(rollout.shape, code),
        pltpu.VMEM(projection.shape, code),
        pltpu.VMEM(location.shape, jnp.int32),
        pltpu.VMEM((slots, own_blocks), jnp.int32),
        pltpu.VMEM((1, own_blocks), jnp.int32),
        pltpu.VMEM(own_pairs, jnp.int32),
        slot,
        pltpu.VMEM((share, blk), wide),
        pltpu.VMEM((n, share, blk), wide),
        frames,
        pltpu.VMEM((own_blocks, blk), wide),
        pltpu.VMEM((reps,) + own_pairs, jnp.int32),
    ]
    held = sum(math.prod(a.shape) * a.dtype.itemsize for a in scratch)
    lists = jax.ShapeDtypeStruct((8, places + 128), jnp.int32)
    scratch += [
        pltpu.SMEM(lists.shape, jnp.int32),
        dma((2, hops, CHUNKS)), dma((2, hops, CHUNKS)),
        dma((2, hops + 1, CHUNKS)), dma((2, hops + 1, CHUNKS)),
        dma((n - 1,)), dma((n - 1,)),
        dma((3, reps - 1)), dma((3, reps - 1)),
        dma((7,)),
    ]
    return pl.pallas_call(
        functools.partial(gather_kernel, n, reps, slots),
        out_shape=[jax.ShapeDtypeStruct((places * blk, blk), wide), lists],
        in_specs=[hbm] * 6,
        out_specs=[vmem] * 2,
        scratch_shapes=scratch,
        compiler_params=pltpu.CompilerParams(
            collective_id=0, has_side_effects=True, vmem_limit_bytes=held + 3 * MIB
        ),
        name="gather_costs",
    )(*(
        pltpu.with_memory_space_constraint(a, pltpu.HBM)
        for a in (demo, rollout, projection, pair_block.T, pair_count[None, :], location)
    ))


def column_kernel(n, reps, sums, *refs):
    if reps:
        out, both, from_twin, added, landed, full, held, *sems, rep_send, rep_recv = refs
    else:
        out, from_twin, added, landed, full, *sems = refs
    first_send, first_recv, second_send, second_recv, twin_send, twin_recv = sems
    me = lax.axis_index("roll")
    chips = n // 2
    core = lax.rem(me, 2)
    chip = me // 2
    twin = {"roll": me + 1 - 2 * core}
    peers = [lax.rem(chip + d, chips) for d in range(1, chips)]
    partners = [{"roll": peer * 2 + core} for peer in peers]
    twins = others("rep", reps) if reps else []
    greet([twin] + partners + twins)

    def remote(source, target, sends, recvs, device):
        copy = pltpu.make_async_remote_copy(
            src_ref=source, dst_ref=target, send_sem=sends, recv_sem=recvs, device_id=device, device_id_type=MESH
        )
        copy.start()
        return copy

    across = [
        remote(sums.at[c, 1 - core], from_twin.at[c], twin_send.at[c], twin_recv.at[c], twin) for c in range(chips)
    ]
    for copy in across:
        copy.wait_recv()
    added[...] = from_twin[...] + sums[:, core]
    firsts = [
        remote(added.at[peer], landed.at[d], first_send.at[d], first_recv.at[d], partners[d])
        for d, peer in enumerate(peers)
    ]
    total = added[chip]
    for d, copy in enumerate(firsts):
        copy.wait_recv()
        total = total + landed[d]
    pot = SHIFT - jnp.log2(total + FLOOR)
    full[core, chip] = pot
    seconds = [
        remote(full.at[core, chip], full.at[core, chip], second_send.at[d], second_recv.at[d], partner)
        for d, partner in enumerate(partners)
    ]
    if reps:
        part = lax.axis_index("rep")
        held[part] = pot * (1.0 / SCALE)
        rep_copies = [
            remote(held.at[part], held.at[part], rep_send.at[d], rep_recv.at[d], partner)
            for d, partner in enumerate(twins)
        ]
    for copy in seconds:
        copy.wait_recv()
    last = remote(full.at[core], full.at[core], twin_send.at[chips], twin_recv.at[chips], twin)
    out[:, core] = full[core]
    last.wait_recv()
    out[:, 1 - core] = full[1 - core]
    for copy in across + firsts + seconds + [last]:
        copy.wait_send()
    if reps:
        for copy in rep_copies:
            copy.wait()
        both[...] = held[...]


def column_potentials(n, reps, sums, call):
    last = call == ITERS - 1
    share, blk = sums.shape[0] // n, sums.shape[1]
    if n > DIRECT:
        pot = SHIFT - jnp.log2(lax.psum(sums, "roll") + FLOOR)
        if not last:
            return pot, None
        mine = lax.dynamic_slice_in_dim(pot, lax.axis_index("roll") * share, share, 0)
        return pot, lax.all_gather(mine, "rep") / SCALE
    chips = n // 2
    sums = sums.reshape(chips, 2, share, blk)
    dma = pltpu.SemaphoreType.DMA
    vmem = pl.BlockSpec(memory_space=pltpu.VMEM)
    both = (reps, share, blk)
    outs = [jax.ShapeDtypeStruct(sums.shape, sums.dtype)]
    scratch = [pltpu.VMEM(shape + (share, blk), jnp.float32) for shape in ((chips,), (chips,), (chips - 1,), (2, chips))]
    if last:
        outs.append(jax.ShapeDtypeStruct(both, sums.dtype))
        scratch.append(pltpu.VMEM(both, jnp.float32))
    scratch += [dma((chips - 1,))] * 4 + [dma((chips + 1,))] * 2
    if last:
        scratch += [dma((reps - 1,))] * 2
    out = pl.pallas_call(
        functools.partial(column_kernel, n, reps if last else 0),
        out_shape=outs,
        in_specs=[vmem],
        out_specs=[vmem] * len(outs),
        scratch_shapes=scratch,
        compiler_params=pltpu.CompilerParams(
            collective_id=1 + call, has_side_effects=True, vmem_limit_bytes=MIB
        ),
        name="column_exchange_%d" % call,
    )(sums)
    return out[0].reshape(n * share, blk), out[1] if last else None


def row_kernel(reps, last, sums, *refs):
    outs, (landed, send_sem, recv_sem) = refs[:-3], refs[-3:]
    part = lax.axis_index("rep")
    partners = others("rep", reps)
    greet(partners)
    copies = []
    for d, partner in enumerate(partners):
        copy = pltpu.make_async_remote_copy(
            src_ref=sums, dst_ref=landed.at[d], send_sem=send_sem.at[d], recv_sem=recv_sem.at[d],
            device_id=partner, device_id_type=MESH,
        )
        copy.start()
        copies.append(copy)
    for copy in copies:
        copy.wait_recv()
    if last:
        heights, weighted = (
            sum((landed[d, k, part] for d in range(reps - 1)), sums[k, part]) for k in range(2)
        )
        heights = heights + FLOOR
        outs[0][...] = -(weighted + UNMATCHED * FLOOR) / heights
        outs[1][...] = (SHIFT - jnp.log2(heights)) * (1.0 / SCALE)
    else:
        total = sum((landed[d, 0] for d in range(reps - 1)), sums[0])
        outs[0][...] = SHIFT - jnp.log2(total + FLOOR)
    for copy in copies:
        copy.wait_send()


def row_totals(reps, sums, call):
    last = call == ITERS - 1
    sums = sums.reshape(sums.shape[0], reps, -1, sums.shape[2])
    dma = pltpu.SemaphoreType.DMA((reps - 1,))
    vmem = pl.BlockSpec(memory_space=pltpu.VMEM)
    shapes = [sums.shape[2:]] * 2 if last else [sums.shape[1:]]
    return pl.pallas_call(
        functools.partial(row_kernel, reps, last),
        out_shape=[jax.ShapeDtypeStruct(shape, sums.dtype) for shape in shapes],
        in_specs=[vmem],
        out_specs=[vmem] * len(shapes),
        scratch_shapes=[pltpu.VMEM((reps - 1,) + sums.shape, jnp.float32), dma, dma],
        compiler_params=pltpu.CompilerParams(
            collective_id=1 + ITERS + call, has_side_effects=True, vmem_limit_bytes=2 * MIB
        ),
        name="row_exchange_%d" % call,
    )(sums)


def body(rollout, demo, projection, location, pair_block, pair_count):
    own_blocks = pair_block.shape[0]
    blk = rollout.shape[0] // own_blocks
    n = lax.axis_size("roll")
    reps = lax.axis_size("rep")
    demo_count = demo.shape[0] // blk
    share = demo_count // reps
    sizes = (reps * own_blocks, n * share, blk)
    stored = n <= DIRECT
    if stored:
        costs, lists = gathered(n, reps, demo, rollout, projection, pair_block, pair_count, location)
        data = (costs,)
    else:
        part = lax.axis_index("rep")
        own_demo = lax.dynamic_slice_in_dim(demo, part * (share * blk), share * blk, 0)
        own_v = project(own_demo, projection)
        own_u = project(rollout, projection)
        flipped = own_v.reshape(share, blk, -1).transpose(0, 2, 1).reshape(-1, blk)
        v, vnorm = (lax.all_gather(a, "roll") for a in (flipped, norms(own_v, blk)))
        u, unorm = (lax.all_gather(a, "rep") for a in (own_u, norms(own_u, blk)))
        pairs, counts = (lax.all_gather(a, "rep", tiled=True) for a in (pair_block, pair_count))
        lists = listed(pairs, counts, location, demo_count, share, part)
        data = tuple(a.reshape(-1, a.shape[-1]) for a in (u, v, unorm, vnorm))

    roll_pot = None
    for iteration in range(ITERS):
        sums = run_pass("column", sizes, lists, data, roll_pot, stored)[0]
        demo_pot, held_pot = column_potentials(n, reps, sums, iteration)
        kind = "final" if iteration == ITERS - 1 else "row"
        sums = run_pass(kind, sizes, lists, data, demo_pot, stored)[0]
        results = row_totals(reps, sums, iteration)
        roll_pot = results[0].reshape(-1, blk) if kind == "row" else None
    return results[0].reshape(-1), results[1].reshape(-1), held_pot.reshape(-1)


def solution(mesh):
    placed = (
        P(("roll", "rep"), None),
        P("roll", None),
        P(),
        P(),
        P(("roll", "rep"), None),
        P(("roll", "rep")),
    )
    return jax.shard_map(
        body,
        mesh=mesh,
        in_specs=placed,
        out_specs=(P(("roll", "rep")), P(("roll", "rep")), P("roll")),
        check_vma=False,
    )
```
